32 devices in a mesh: rows: 16 (over z, x, core), grp: 2 (over y).
Axes of the slice: x: 2, y: 2, z: 4, core: 2. Of those that a mesh axis runs over, the one named last changes fastest.
Arguments:
- snapshots: float32 [131072, 256], P(('rows', 'grp'))
- blocks: bfloat16 [1024, 16, 128, 128], P(('rows', 'grp')), may hold values from -48 to 48
- columns: int32 [1024, 16], P(('rows', 'grp')), may hold values from 0 to 63
Outputs:
- projected: float32 [256, 256], replicated
- scaled_factor: float32 [256, 256], replicated
The draws below stay inside these ranges and needn't reach their ends.
Inputs may be any that keep to these rules, and one draw needn't show every extreme that they name: `columns`: each stored block couples its block row to a block row of the same group of 2 * 32 consecutive block rows.
All inputs are finite; a program needn't handle non-finite values.
Results may differ from the reference program's by a relative error of at most 0.003.
Values may be sent and summed in bfloat16 or wider, within the bound.
A program may use at most 192 MiB of HBM per device.

```python
import math
import jax
import jax.numpy as jnp
from jax import lax

K = 256
BLK = 128
NNZB = 16
NBLK = 32
ROWS = 131072
NBR = 1024
N_GRP = 2


def draw_snapshots(key, part):
    key_base, key_col, key_row = jax.random.split(key, 3)
    base = jax.random.normal(key_base, (ROWS, K), jnp.float32)
    col_scale = jnp.exp(jax.random.uniform(key_col, (1, K), jnp.float32, 0.0, math.log(10.0)))
    row_scale = jnp.exp(jax.random.uniform(key_row, (ROWS, 1), jnp.float32, 0.0, math.log(10.0)))
    values = base * col_scale * row_scale
    return values


def place_ends(array, stream_key, smallest, high):
    longest = array.shape.index(max(array.shape))
    spots = []
    for shift in (0, 1):
        where = [jax.random.randint(jax.random.fold_in(stream_key, axis), (), 0, length) for axis, length in enumerate(array.shape)]
        where[longest] = (where[longest] + shift) % array.shape[longest]
        spots.append(tuple(where))
    return array.at[spots[0]].set(smallest).at[spots[1]].set(high)


def block_levels(stream_key, dims, pieces, smallest, top_value):
    def one(axis_at, parts):
        heights = jax.random.uniform(jax.random.fold_in(jax.random.fold_in(stream_key, 6), axis_at), (parts,), jnp.float32, smallest / len(pieces), top_value / len(pieces))
        return jnp.repeat(jnp.exp(heights), dims[axis_at] // parts).reshape((-1,) + (1,) * (len(dims) - axis_at - 1))

    factor_of = one(*pieces[0])
    for cut in pieces[1:]:
        factor_of = factor_of * one(*cut)
    return factor_of


def centred(own_key, dims, deviation, most, cuts=(), held_as=jnp.bfloat16):
    loudness = block_levels(own_key, dims, cuts, -0.22, 0.18) if cuts else 1.0
    entries = jax.random.normal(own_key, dims, jnp.float32) * deviation * loudness
    return jnp.minimum(jnp.maximum(entries, -most), most).astype(held_as)


def setup_inputs(seed: int = 0) -> dict:
    splits = jax.random.split(jax.random.key(seed), 4)
    return {
        "snapshots": draw_snapshots(jax.random.fold_in(splits[3], 71), 0),
        "blocks": centred(splits[1], (NBR, NNZB, BLK, BLK), ((ROWS // (BLK * NNZB)) ** 0.5), 48.0, ((0, 32),)),
        "columns": place_ends(jax.random.randint(splits[2], (NBR, NNZB), 0, N_GRP * NBLK), jax.random.fold_in(splits[2], 1), 0, (N_GRP * NBLK) - 1).astype(jnp.int32),
    }


def upper_inverse(factor):
    size = factor.shape[0]
    unit_rows = jnp.eye(size, dtype=factor.dtype)

    def substitute(count, inverse):
        index = (size - 1 - count).astype(jnp.int32)
        frow = lax.dynamic_slice_in_dim(factor, index, 1, 0)
        unit = lax.dynamic_slice_in_dim(unit_rows, index, 1, 0)
        pivot = lax.dynamic_slice(factor, (index, index), (1, 1))
        fresh = (unit - jnp.dot(frow, inverse, precision=lax.Precision.HIGHEST)) / pivot
        return lax.dynamic_update_slice_in_dim(inverse, fresh, index, 0)
    return lax.fori_loop(jnp.int32(0), jnp.int32(size), substitute, jnp.zeros_like(factor))

def reference(snapshots, blocks, columns):
    highest = lax.Precision.HIGHEST
    gram = lax.dot_general(snapshots.astype(jnp.float32), snapshots.astype(jnp.float32), (((0,), (0,)), ((), ())), precision=highest, preferred_element_type=jnp.float32)
    factor = jnp.linalg.cholesky(gram).T
    inverse = upper_inverse(factor)
    basis = jnp.dot(snapshots, inverse, precision=highest)
    basis_half = basis.astype(jnp.bfloat16)
    half_blocks = basis_half.reshape(NBR, BLK, K)
    group_len = N_GRP * NBLK
    base = jnp.arange(NBR, dtype=jnp.int32) // group_len * group_len
    target = (base[:, None] + columns).astype(jnp.int32)
    block_groups = blocks.reshape(NBR // NBLK, NBLK, NNZB, BLK, BLK)
    target_groups = target.reshape(NBR // NBLK, NBLK, NNZB)

    def one_group(pair):
        group_blocks, group_target = pair
        picked = half_blocks[group_target]
        return jnp.einsum('bjrc,bjck->brk', group_blocks.astype(jnp.float32), picked.astype(jnp.float32))
    image = lax.map(one_group, (block_groups, target_groups)).reshape(ROWS, K)
    projected = lax.dot_general(basis.astype(jnp.float32), image.astype(jnp.float32), (((0,), (0,)), ((), ())), precision=highest, preferred_element_type=jnp.float32)
    scaled_factor = factor / math.sqrt(ROWS)
    return (projected, scaled_factor)
```

```python
import functools
import math

import jax
import jax.numpy as jnp
from jax import lax
from jax.experimental import pallas as pl
from jax.experimental.pallas import tpu as pltpu
from jax.sharding import PartitionSpec as P

HIGHEST = lax.Precision.HIGHEST
LANES = 128
SUB = 8


def dot(left, right, dims=((1,), (0,)), precision=HIGHEST):
    return lax.dot_general(
        left, right, (dims, ((), ())), precision=precision, preferred_element_type=jnp.float32
    )


def across(value, lane, shape):
    return jnp.broadcast_to(value[..., lane : lane + 1], shape)


def eliminate(head, tail):
    tiles = head.shape[0]
    one = (SUB, LANES)
    for tile in range(tiles):
        base = tile * SUB
        rows_h = [jnp.broadcast_to(head[tile, k : k + 1, :], one) for k in range(SUB)]
        rows_t = [jnp.broadcast_to(tail[tile, k : k + 1, :], one) for k in range(SUB)]
        d = {}
        for k in range(SUB):
            for i in range(k, SUB):
                d[k, i] = across(rows_h[k], base + i, one)
        later = tiles - tile - 1
        if later:
            rest_h = head[tile + 1 :]
            rest_t = tail[tile + 1 :]
            low = [across(rest_h, base + k, (later, SUB, LANES)) for k in range(SUB)]
        for k in range(SUB):
            scale = lax.rsqrt(d[k, k])
            for i in range(k + 1, SUB):
                d[k, i] = d[k, i] * scale
            rows_h[k] = rows_h[k] * scale
            rows_t[k] = rows_t[k] * scale
            for i in range(k + 1, SUB):
                for m in range(i, SUB):
                    d[i, m] = d[i, m] - d[k, i] * d[k, m]
                rows_h[i] = rows_h[i] - d[k, i] * rows_h[k]
                rows_t[i] = rows_t[i] - d[k, i] * rows_t[k]
            if later:
                low[k] = low[k] * scale[None]
                for m in range(k + 1, SUB):
                    low[m] = low[m] - low[k] * d[k, m][None]
                rest_h = rest_h - low[k] * rows_h[k][None]
                rest_t = rest_t - low[k] * rows_t[k][None]
            head[tile, k : k + 1, :] = rows_h[k][:1]
            tail[tile, k : k + 1, :] = rows_t[k][:1]
        if later:
            head[tile + 1 :] = rest_h
            tail[tile + 1 :] = rest_t


def factor_kernel(gram_ref, factor_ref, inverse_ref, head, tail):
    size = gram_ref.shape[0]
    n = LANES
    row = lax.broadcasted_iota(jnp.int32, (n, n), 0)
    col = lax.broadcasted_iota(jnp.int32, (n, n), 1)
    eye = jnp.where(row == col, 1.0, 0.0).astype(jnp.float32)
    tiles = (n // SUB, SUB, n)
    count = size // n

    for b in range(count):
        here = slice(b * n, (b + 1) * n)
        square = gram_ref[here, here]
        for a in range(b):
            above = factor_ref[a * n : (a + 1) * n, here]
            square = square - dot(above, above, ((0,), (0,)))
        head[...] = square.reshape(tiles)
        tail[...] = eye.reshape(tiles)
        eliminate(head, tail)
        lower = jnp.where(row >= col, tail[...].reshape(n, n), 0.0)
        factor_ref[here, here] = jnp.where(row <= col, head[...].reshape(n, n), 0.0)
        upper = lower.T
        inverse_ref[here, here] = upper
        for c in range(b + 1, count):
            there = slice(c * n, (c + 1) * n)
            rest = gram_ref[here, there]
            for a in range(b):
                span = slice(a * n, (a + 1) * n)
                rest = rest - dot(factor_ref[span, here], factor_ref[span, there], ((0,), (0,)))
            factor_ref[here, there] = dot(lower, rest)
            factor_ref[there, here] = jnp.zeros((n, n), jnp.float32)
            inverse_ref[there, here] = jnp.zeros((n, n), jnp.float32)
        for a in range(b):
            span = slice(a * n, (a + 1) * n)
            total = jnp.zeros((n, n), jnp.float32)
            for m in range(a, b):
                mid = slice(m * n, (m + 1) * n)
                total = total + dot(inverse_ref[span, mid], factor_ref[mid, here])
            inverse_ref[span, here] = -dot(total, upper)


def factorize(gram):
    size = gram.shape[0]
    square = jax.ShapeDtypeStruct((size, size), jnp.float32)
    return pl.pallas_call(
        factor_kernel,
        out_shape=(square, square),
        in_specs=[pl.BlockSpec(memory_space=pltpu.VMEM)],
        out_specs=(pl.BlockSpec(memory_space=pltpu.VMEM),) * 2,
        scratch_shapes=[pltpu.VMEM((LANES // SUB, SUB, LANES), jnp.float32)] * 2,
        compiler_params=pltpu.CompilerParams(vmem_limit_bytes=16 * 2**20),
        name="factorize",
    )(gram)


def split(value):
    high = value.astype(jnp.bfloat16)
    return high, (value - high.astype(jnp.float32)).astype(jnp.bfloat16)


def project_kernel(per_step, columns_ref, blocks_ref, basis_ref, window_ref, out_ref):
    step = pl.program_id(0)
    stored, block_len = blocks_ref.shape[1], blocks_ref.shape[2]

    @pl.when(step == 0)
    def _():
        out_ref[...] = jnp.zeros_like(out_ref)

    images = []
    for r in range(per_step):
        picked = []
        for j in range(stored):
            at = columns_ref[step * per_step + r, j] * block_len
            picked.append(window_ref[pl.ds(pl.multiple_of(at, block_len), block_len), :])
        left = jnp.concatenate([blocks_ref[r, j] for j in range(stored)], axis=1)
        right = jnp.concatenate(picked, axis=0)
        images.append(jnp.dot(left, right, preferred_element_type=jnp.float32))
    image = jnp.concatenate(images, axis=0)
    image_high, image_low = split(image)
    basis_high, basis_low = split(basis_ref[...])
    rows = ((0,), (0,))
    term = dot(basis_high, image_high, rows, None)
    term = term + dot(basis_high, image_low, rows, None)
    term = term + dot(basis_low, image_high, rows, None)
    out_ref[...] += term


def project(columns, blocks, basis, window):
    block_rows, stored, block_len, _ = blocks.shape
    width = basis.shape[1]
    per_step = 2
    grid_spec = pltpu.PrefetchScalarGridSpec(
        num_scalar_prefetch=1,
        grid=(block_rows // per_step,),
        in_specs=[
            pl.BlockSpec((per_step, stored, block_len, block_len), lambda i, c: (i, 0, 0, 0)),
            pl.BlockSpec((per_step * block_len, width), lambda i, c: (i, 0)),
            pl.BlockSpec(window.shape, lambda i, c: (0, 0)),
        ],
        out_specs=pl.BlockSpec((width, width), lambda i, c: (0, 0)),
    )
    return pl.pallas_call(
        functools.partial(project_kernel, per_step),
        grid_spec=grid_spec,
        out_shape=jax.ShapeDtypeStruct((width, width), jnp.float32),
        compiler_params=pltpu.CompilerParams(vmem_limit_bytes=40 * 2**20),
        name="project",
    )(columns, blocks, basis, window)


def local(snapshots, blocks, columns):
    axes = ("rows", "grp")
    gram = lax.psum(dot(snapshots, snapshots, ((0,), (0,))), axes)
    factor, inverse = factorize(gram)
    basis = dot(snapshots, inverse)
    basis_half = basis.astype(jnp.bfloat16)
    window = lax.all_gather(basis_half, "grp", axis=0, tiled=True)
    partial_terms = project(columns, blocks, basis, window)
    projected = lax.psum(partial_terms, axes)
    total_rows = snapshots.shape[0] * lax.axis_size(axes)
    return projected, factor / math.sqrt(total_rows)


def solution(mesh):
    return jax.shard_map(
        local,
        mesh=mesh,
        in_specs=(
            P(("rows", "grp"), None),
            P(("rows", "grp"), None, None, None),
            P(("rows", "grp"), None),
        ),
        out_specs=(P(), P()),
        check_vma=False,
    )
```

```python
import functools
import math

import jax
import jax.numpy as jnp
from jax import lax
from jax.experimental import pallas as pl
from jax.experimental.pallas import tpu as pltpu
from jax.sharding import PartitionSpec as P

HIGHEST = lax.Precision.HIGHEST
LANES = 128
SUB = 8
MESH = pl.DeviceIdType.MESH


def dot(left, right, dims=((1,), (0,)), precision=HIGHEST):
    return lax.dot_general(
        left, right, (dims, ((), ())), precision=precision, preferred_element_type=jnp.float32
    )


def across(value, lane, shape):
    return jnp.broadcast_to(value[..., lane : lane + 1], shape)


def eliminate(head, tail):
    tiles = head.shape[0]
    one = (SUB, LANES)
    for tile in range(tiles):
        base = tile * SUB
        rows_h = [jnp.broadcast_to(head[tile, k : k + 1, :], one) for k in range(SUB)]
        rows_t = [jnp.broadcast_to(tail[tile, k : k + 1, :], one) for k in range(SUB)]
        d = {}
        for k in range(SUB):
            for i in range(k, SUB):
                d[k, i] = across(rows_h[k], base + i, one)
        later = tiles - tile - 1
        if later:
            rest_h = head[tile + 1 :]
            rest_t = tail[tile + 1 :]
            low = [across(rest_h, base + k, (later, SUB, LANES)) for k in range(SUB)]
        for k in range(SUB):
            scale = lax.rsqrt(d[k, k])
            for i in range(k + 1, SUB):
                d[k, i] = d[k, i] * scale
            rows_h[k] = rows_h[k] * scale
            rows_t[k] = rows_t[k] * scale
            for i in range(k + 1, SUB):
                for m in range(i, SUB):
                    d[i, m] = d[i, m] - d[k, i] * d[k, m]
                rows_h[i] = rows_h[i] - d[k, i] * rows_h[k]
                rows_t[i] = rows_t[i] - d[k, i] * rows_t[k]
            if later:
                low[k] = low[k] * scale[None]
                for m in range(k + 1, SUB):
                    low[m] = low[m] - low[k] * d[k, m][None]
                rest_h = rest_h - low[k] * rows_h[k][None]
                rest_t = rest_t - low[k] * rows_t[k][None]
            head[tile, k : k + 1, :] = rows_h[k][:1]
            tail[tile, k : k + 1, :] = rows_t[k][:1]
        if later:
            head[tile + 1 :] = rest_h
            tail[tile + 1 :] = rest_t


def factor_kernel(gram_ref, factor_ref, inverse_ref, head, tail):
    size = gram_ref.shape[0]
    n = LANES
    row = lax.broadcasted_iota(jnp.int32, (n, n), 0)
    col = lax.broadcasted_iota(jnp.int32, (n, n), 1)
    eye = jnp.where(row == col, 1.0, 0.0).astype(jnp.float32)
    tiles = (n // SUB, SUB, n)
    count = size // n

    for b in range(count):
        here = slice(b * n, (b + 1) * n)
        square = gram_ref[here, here]
        for a in range(b):
            above = factor_ref[a * n : (a + 1) * n, here]
            square = square - dot(above, above, ((0,), (0,)))
        head[...] = square.reshape(tiles)
        tail[...] = eye.reshape(tiles)
        eliminate(head, tail)
        lower = jnp.where(row >= col, tail[...].reshape(n, n), 0.0)
        factor_ref[here, here] = jnp.where(row <= col, head[...].reshape(n, n), 0.0)
        upper = lower.T
        inverse_ref[here, here] = upper
        for c in range(b + 1, count):
            there = slice(c * n, (c + 1) * n)
            rest = gram_ref[here, there]
            for a in range(b):
                span = slice(a * n, (a + 1) * n)
                rest = rest - dot(factor_ref[span, here], factor_ref[span, there], ((0,), (0,)))
            factor_ref[here, there] = dot(lower, rest)
            factor_ref[there, here] = jnp.zeros((n, n), jnp.float32)
            inverse_ref[there, here] = jnp.zeros((n, n), jnp.float32)
        for a in range(b):
            span = slice(a * n, (a + 1) * n)
            total = jnp.zeros((n, n), jnp.float32)
            for m in range(a, b):
                mid = slice(m * n, (m + 1) * n)
                total = total + dot(inverse_ref[span, mid], factor_ref[mid, here])
            inverse_ref[span, here] = -dot(total, upper)


def factorize(gram):
    size = gram.shape[0]
    square = jax.ShapeDtypeStruct((size, size), jnp.float32)
    return pl.pallas_call(
        factor_kernel,
        out_shape=(square, square),
        in_specs=[pl.BlockSpec(memory_space=pltpu.VMEM)],
        out_specs=(pl.BlockSpec(memory_space=pltpu.VMEM),) * 2,
        scratch_shapes=[pltpu.VMEM((LANES // SUB, SUB, LANES), jnp.float32)] * 2,
        compiler_params=pltpu.CompilerParams(vmem_limit_bytes=16 * 2**20),
        name="factorize",
    )(gram)


def split(value):
    high = value.astype(jnp.bfloat16)
    return high, (value - high.astype(jnp.float32)).astype(jnp.bfloat16)


def sum_kernel(axes, sizes, x_ref, out_ref, pair, own, slots, held, pair_sems, scatter_sems, gather_sems, last_sems):
    rows_axis, grp_axis = axes
    grps = sizes[1]
    chips = x_ref.shape[1]
    me_row, me_grp = lax.axis_index(rows_axis), lax.axis_index(grp_axis)
    core = lax.rem(me_row, 2)
    me = (me_row // 2) * grps + me_grp

    def chip(offset):
        other = lax.rem(me + offset, chips)
        return other, {rows_axis: (other // grps) * 2 + core, grp_axis: lax.rem(other, grps)}

    mate = {rows_axis: me_row + 1 - 2 * core, grp_axis: me_grp}

    barrier = pltpu.get_barrier_semaphore()
    pl.semaphore_signal(barrier, inc=1, device_id=mate, device_id_type=MESH)

    def greet(offset, carry):
        pl.semaphore_signal(barrier, inc=1, device_id=chip(offset)[1], device_id_type=MESH)
        return carry

    lax.fori_loop(1, chips, greet, 0)
    pl.semaphore_wait(barrier, chips)

    first = pltpu.make_async_remote_copy(
        src_ref=x_ref.at[1 - core], dst_ref=pair, send_sem=pair_sems.at[0], recv_sem=pair_sems.at[1],
        device_id=mate, device_id_type=MESH)
    first.start()
    first.wait()
    own[...] = x_ref[core] + pair[...]

    def scatter(offset):
        other, where = chip(offset)
        return pltpu.make_async_remote_copy(
            src_ref=own.at[other], dst_ref=slots.at[offset],
            send_sem=scatter_sems.at[0, offset], recv_sem=scatter_sems.at[1, offset],
            device_id=where, device_id_type=MESH)

    def gather(offset):
        _, where = chip(offset)
        return pltpu.make_async_remote_copy(
            src_ref=held.at[core, me], dst_ref=held.at[core, me],
            send_sem=gather_sems.at[0, offset], recv_sem=gather_sems.at[1, offset],
            device_id=where, device_id_type=MESH)

    def each(make, act):
        def body(offset, carry):
            getattr(make(offset), act)()
            return carry
        lax.fori_loop(1, chips, body, 0)

    each(scatter, "start")
    slots[0] = own[me]
    each(scatter, "wait_recv")
    held[core, me] = jnp.sum(slots[...], axis=0)
    each(gather, "start")
    each(scatter, "wait_send")
    each(gather, "wait_recv")
    last = pltpu.make_async_remote_copy(
        src_ref=held.at[core], dst_ref=held.at[core], send_sem=last_sems.at[0], recv_sem=last_sems.at[1],
        device_id=mate, device_id_type=MESH)
    last.start()
    each(gather, "wait_send")
    last.wait()
    out_ref[...] = held[...]


def device_sum(value, axes):
    sizes = tuple(lax.axis_size(axis) for axis in axes)
    chips = sizes[0] * sizes[1] // 2
    height, width = value.shape
    piece = height // (2 * chips)
    shape = (2, chips, piece, width)
    f32 = jnp.float32
    out = pl.pallas_call(
        functools.partial(sum_kernel, axes, sizes),
        out_shape=jax.ShapeDtypeStruct(shape, f32),
        in_specs=[pl.BlockSpec(memory_space=pltpu.VMEM)],
        out_specs=pl.BlockSpec(memory_space=pltpu.VMEM),
        scratch_shapes=[
            pltpu.VMEM((chips, piece, width), f32),
            pltpu.VMEM((chips, piece, width), f32),
            pltpu.VMEM((chips, piece, width), f32),
            pltpu.VMEM(shape, f32),
            pltpu.SemaphoreType.DMA((2,)),
            pltpu.SemaphoreType.DMA((2, chips)),
            pltpu.SemaphoreType.DMA((2, chips)),
            pltpu.SemaphoreType.DMA((2,)),
        ],
        compiler_params=pltpu.CompilerParams(collective_id=0, has_side_effects=True),
        name="device_sum",
    )(value.reshape(shape))
    return out.reshape(height, width)


def project_kernel(per_step, columns_ref, blocks_ref, basis_ref, *refs):
    *parts, out_ref, window_ref, sems = refs
    step = pl.program_id(0)
    stored, block_len = blocks_ref.shape[1], blocks_ref.shape[2]

    @pl.when(step == 0)
    def _():
        out_ref[...] = jnp.zeros_like(out_ref)
        copies, at = [], 0
        for index, part in enumerate(parts):
            size = part.shape[0]
            copies.append(pltpu.make_async_copy(part, window_ref.at[pl.ds(at, size)], sems.at[index]))
            at += size
        for copy in copies:
            copy.start()
        for copy in copies:
            copy.wait()

    images = []
    for r in range(per_step):
        picked = []
        for j in range(stored):
            at = columns_ref[step * per_step + r, j] * block_len
            picked.append(window_ref[pl.ds(pl.multiple_of(at, block_len), block_len), :])
        left = jnp.concatenate([blocks_ref[r, j] for j in range(stored)], axis=1)
        right = jnp.concatenate(picked, axis=0)
        images.append(jnp.dot(left, right, preferred_element_type=jnp.float32))
    image = jnp.concatenate(images, axis=0)
    image_high, image_low = split(image)
    basis_high, basis_low = split(basis_ref[...])
    rows = ((0,), (0,))
    term = dot(basis_high, image_high, rows, None)
    term = term + dot(basis_high, image_low, rows, None)
    term = term + dot(basis_low, image_high, rows, None)
    out_ref[...] += term


def project(columns, blocks, basis, parts):
    block_rows, stored, block_len, _ = blocks.shape
    width = basis.shape[1]
    per_step = 2
    depth = sum(part.shape[0] for part in parts)
    grid_spec = pltpu.PrefetchScalarGridSpec(
        num_scalar_prefetch=1,
        grid=(block_rows // per_step,),
        in_specs=[
            pl.BlockSpec((per_step, stored, block_len, block_len), lambda i, c: (i, 0, 0, 0)),
            pl.BlockSpec((per_step * block_len, width), lambda i, c: (i, 0)),
        ] + [pl.BlockSpec(memory_space=pl.ANY)] * len(parts),
        out_specs=pl.BlockSpec((width, width), lambda i, c: (0, 0)),
        scratch_shapes=[
            pltpu.VMEM((depth, width), jnp.bfloat16),
            pltpu.SemaphoreType.DMA((len(parts),)),
        ],
    )
    return pl.pallas_call(
        functools.partial(project_kernel, per_step),
        grid_spec=grid_spec,
        out_shape=jax.ShapeDtypeStruct((width, width), jnp.float32),
        compiler_params=pltpu.CompilerParams(vmem_limit_bytes=40 * 2**20),
        name="project",
    )(columns, blocks, basis, *parts)


def ring(value, axis):
    size = lax.axis_size(axis)
    for shift in range(1, size):
        yield lax.ppermute(value, axis, [((d + shift) % size, d) for d in range(size)])


def local(snapshots, blocks, columns):
    axes = ("rows", "grp")
    height = snapshots.shape[0]
    early = height // 2
    raws = list(ring(snapshots[:early], "grp"))
    gram = device_sum(dot(snapshots, snapshots, ((0,), (0,))), axes)
    factor, inverse = factorize(gram)
    basis = dot(snapshots, inverse)
    basis_half = basis.astype(jnp.bfloat16)
    lates = list(ring(basis_half[early:], "grp"))
    parts = [basis_half]
    for raw, late in zip(raws, lates):
        parts += [dot(raw, inverse).astype(jnp.bfloat16), late]
    block_rows = blocks.shape[0]
    size = lax.axis_size("grp")
    turned = lax.rem(columns + (size - lax.axis_index("grp")) * block_rows, size * block_rows)
    projected = device_sum(project(turned, blocks, basis, parts), axes)
    total_rows = height * lax.axis_size(axes)
    return projected, factor / math.sqrt(total_rows)


def solution(mesh):
    return jax.shard_map(
        local,
        mesh=mesh,
        in_specs=(
            P(("rows", "grp"), None),
            P(("rows", "grp"), None, None, None),
            P(("rows", "grp"), None),
        ),
        out_specs=(P(), P()),
        check_vma=False,
    )
```

```python
import functools
import math

import jax
import jax.numpy as jnp
from jax import lax
from jax.experimental import pallas as pl
from jax.experimental.pallas import tpu as pltpu
from jax.sharding import PartitionSpec as P

HIGHEST = lax.Precision.HIGHEST
LANES = 128
SUB = 8
MESH = pl.DeviceIdType.MESH


def dot(left, right, dims=((1,), (0,)), precision=HIGHEST):
    return lax.dot_general(
        left, right, (dims, ((), ())), precision=precision, preferred_element_type=jnp.float32
    )


def across(value, lane, shape):
    return jnp.broadcast_to(value[..., lane : lane + 1], shape)


def eliminate(head, tail):
    tiles = head.shape[0]
    one = (SUB, LANES)
    for tile in range(tiles):
        base = tile * SUB
        rows_h = [jnp.broadcast_to(head[tile, k : k + 1, :], one) for k in range(SUB)]
        rows_t = [jnp.broadcast_to(tail[tile, k : k + 1, :], one) for k in range(SUB)]
        d = {}
        for k in range(SUB):
            for i in range(k, SUB):
                d[k, i] = across(rows_h[k], base + i, one)
        later = tiles - tile - 1
        if later:
            rest_h = head[tile + 1 :]
            rest_t = tail[tile + 1 :]
            low = [across(rest_h, base + k, (later, SUB, LANES)) for k in range(SUB)]
        for k in range(SUB):
            scale = lax.rsqrt(d[k, k])
            for i in range(k + 1, SUB):
                d[k, i] = d[k, i] * scale
            rows_h[k] = rows_h[k] * scale
            rows_t[k] = rows_t[k] * scale
            for i in range(k + 1, SUB):
                for m in range(i, SUB):
                    d[i, m] = d[i, m] - d[k, i] * d[k, m]
                rows_h[i] = rows_h[i] - d[k, i] * rows_h[k]
                rows_t[i] = rows_t[i] - d[k, i] * rows_t[k]
            if later:
                low[k] = low[k] * scale[None]
                for m in range(k + 1, SUB):
                    low[m] = low[m] - low[k] * d[k, m][None]
                rest_h = rest_h - low[k] * rows_h[k][None]
                rest_t = rest_t - low[k] * rows_t[k][None]
            head[tile, k : k + 1, :] = rows_h[k][:1]
            tail[tile, k : k + 1, :] = rows_t[k][:1]
        if later:
            head[tile + 1 :] = rest_h
            tail[tile + 1 :] = rest_t


def factor_kernel(gram_ref, factor_ref, inverse_ref, head, tail):
    size = gram_ref.shape[0]
    n = LANES
    row = lax.broadcasted_iota(jnp.int32, (n, n), 0)
    col = lax.broadcasted_iota(jnp.int32, (n, n), 1)
    eye = jnp.where(row == col, 1.0, 0.0).astype(jnp.float32)
    tiles = (n // SUB, SUB, n)
    count = size // n

    for b in range(count):
        here = slice(b * n, (b + 1) * n)
        square = gram_ref[here, here]
        for a in range(b):
            above = factor_ref[a * n : (a + 1) * n, here]
            square = square - dot(above, above, ((0,), (0,)))
        head[...] = square.reshape(tiles)
        tail[...] = eye.reshape(tiles)
        eliminate(head, tail)
        lower = jnp.where(row >= col, tail[...].reshape(n, n), 0.0)
        factor_ref[here, here] = jnp.where(row <= col, head[...].reshape(n, n), 0.0)
        upper = lower.T
        inverse_ref[here, here] = upper
        for c in range(b + 1, count):
            there = slice(c * n, (c + 1) * n)
            rest = gram_ref[here, there]
            for a in range(b):
                span = slice(a * n, (a + 1) * n)
                rest = rest - dot(factor_ref[span, here], factor_ref[span, there], ((0,), (0,)))
            factor_ref[here, there] = dot(lower, rest)
            factor_ref[there, here] = jnp.zeros((n, n), jnp.float32)
            inverse_ref[there, here] = jnp.zeros((n, n), jnp.float32)
        for a in range(b):
            span = slice(a * n, (a + 1) * n)
            total = jnp.zeros((n, n), jnp.float32)
            for m in range(a, b):
                mid = slice(m * n, (m + 1) * n)
                total = total + dot(inverse_ref[span, mid], factor_ref[mid, here])
            inverse_ref[span, here] = -dot(total, upper)


def factorize(gram):
    size = gram.shape[0]
    square = jax.ShapeDtypeStruct((size, size), jnp.float32)
    return pl.pallas_call(
        factor_kernel,
        out_shape=(square, square),
        in_specs=[pl.BlockSpec(memory_space=pltpu.VMEM)],
        out_specs=(pl.BlockSpec(memory_space=pltpu.VMEM),) * 2,
        scratch_shapes=[pltpu.VMEM((LANES // SUB, SUB, LANES), jnp.float32)] * 2,
        compiler_params=pltpu.CompilerParams(vmem_limit_bytes=16 * 2**20),
        name="factorize",
    )(gram)


def split(value):
    high = value.astype(jnp.bfloat16)
    return high, (value - high.astype(jnp.float32)).astype(jnp.bfloat16)


def mate_of(axes):
    row = lax.axis_index(axes[0])
    return {axes[0]: row + 1 - 2 * lax.rem(row, 2), axes[1]: lax.axis_index(axes[1])}


def greet(barrier, where):
    pl.semaphore_signal(barrier, inc=1, device_id=where, device_id_type=MESH)


def exchange(source, target, sems, where):
    return pltpu.make_async_remote_copy(
        src_ref=source, dst_ref=target, send_sem=sems.at[0], recv_sem=sems.at[1],
        device_id=where, device_id_type=MESH)


def near_kernel(axes, grps, x_ref, out_ref, pair, own, others, pair_sems, grp_sems):
    me_row, me_grp = lax.axis_index(axes[0]), lax.axis_index(axes[1])
    core = lax.rem(me_row, 2)
    mate = mate_of(axes)
    friends = [{axes[0]: me_row, axes[1]: lax.rem(me_grp + shift, grps)} for shift in range(1, grps)]
    barrier = pltpu.get_barrier_semaphore()
    for where in [mate] + friends:
        greet(barrier, where)
    pl.semaphore_wait(barrier, grps)
    first = exchange(x_ref.at[1 - core], pair, pair_sems, mate)
    first.start()
    first.wait()
    own[...] = x_ref[core] + pair[...]
    copies = [exchange(own, others.at[i], grp_sems.at[i], where) for i, where in enumerate(friends)]
    for copy in copies:
        copy.start()
    total = own[...]
    for i, copy in enumerate(copies):
        copy.wait()
        total = total + others[i]
    out_ref[...] = total


def near_sum(value, axes, chips):
    height, width = value.shape
    grps = lax.axis_size(axes[1])
    half = (chips, height // (2 * chips), width)
    f32 = jnp.float32
    return pl.pallas_call(
        functools.partial(near_kernel, axes, grps),
        out_shape=jax.ShapeDtypeStruct(half, f32),
        in_specs=[pl.BlockSpec(memory_space=pltpu.VMEM)],
        out_specs=pl.BlockSpec(memory_space=pltpu.VMEM),
        scratch_shapes=[
            pltpu.VMEM(half, f32),
            pltpu.VMEM(half, f32),
            pltpu.VMEM((grps - 1,) + half, f32),
            pltpu.SemaphoreType.DMA((2,)),
            pltpu.SemaphoreType.DMA((grps - 1, 2)),
        ],
        compiler_params=pltpu.CompilerParams(collective_id=1, has_side_effects=True),
        name="near_sum",
    )(value.reshape((2,) + half))


def sum_kernel(axes, grps, x_ref, out_ref, pair, own, slots, held, pair_sems, scatter_sems, gather_sems, last_sems):
    rows_axis, grp_axis = axes
    chips = own.shape[0]
    me_row, me_grp = lax.axis_index(rows_axis), lax.axis_index(grp_axis)
    core = lax.rem(me_row, 2)
    mate = mate_of(axes)
    whole = grps > 1
    me = (me_row // 2) * grps + me_grp if whole else me_row // 2

    def chip(offset):
        other = lax.rem(me + offset, chips)
        if whole:
            return other, {rows_axis: (other // grps) * 2 + core, grp_axis: lax.rem(other, grps)}
        return other, {rows_axis: other * 2 + core, grp_axis: me_grp}

    barrier = pltpu.get_barrier_semaphore()
    greet(barrier, mate)

    def greet_chip(offset, carry):
        greet(barrier, chip(offset)[1])
        return carry

    lax.fori_loop(1, chips, greet_chip, 0, unroll=chips <= 16)
    pl.semaphore_wait(barrier, chips)

    if whole:
        first = exchange(x_ref.at[1 - core], pair, pair_sems, mate)
        first.start()
        first.wait()
        own[...] = x_ref[core] + pair[...]
    else:
        own[...] = x_ref[...]

    def scatter(offset):
        other, where = chip(offset)
        return pltpu.make_async_remote_copy(
            src_ref=own.at[other], dst_ref=slots.at[offset],
            send_sem=scatter_sems.at[0, offset], recv_sem=scatter_sems.at[1, offset],
            device_id=where, device_id_type=MESH)

    def gather(offset):
        _, where = chip(offset)
        return pltpu.make_async_remote_copy(
            src_ref=held.at[core, me], dst_ref=held.at[core, me],
            send_sem=gather_sems.at[0, offset], recv_sem=gather_sems.at[1, offset],
            device_id=where, device_id_type=MESH)

    def each(make, act):
        def body(offset, carry):
            getattr(make(offset), act)()
            return carry
        lax.fori_loop(1, chips, body, 0, unroll=chips <= 16)

    each(scatter, "start")
    slots[0] = own[me]
    each(scatter, "wait_recv")
    held[core, me] = jnp.sum(slots[...], axis=0)
    each(gather, "start")
    each(scatter, "wait_send")
    each(gather, "wait_recv")
    last = exchange(held.at[core], held.at[core], last_sems, mate)
    last.start()
    each(gather, "wait_send")
    last.wait()
    out_ref[...] = held[...]


def device_sum(value, axes, whole=True):
    grps = lax.axis_size(axes[1]) if whole else 1
    chips = lax.axis_size(axes[0]) // 2 * grps
    height, width = (value.shape[0], value.shape[1]) if whole else (2 * chips * value.shape[1], value.shape[2])
    half = (chips, height // (2 * chips), width)
    f32 = jnp.float32
    out = pl.pallas_call(
        functools.partial(sum_kernel, axes, grps),
        out_shape=jax.ShapeDtypeStruct((2,) + half, f32),
        in_specs=[pl.BlockSpec(memory_space=pltpu.VMEM)],
        out_specs=pl.BlockSpec(memory_space=pltpu.VMEM),
        scratch_shapes=[
            pltpu.VMEM(half, f32),
            pltpu.VMEM(half, f32),
            pltpu.VMEM(half, f32),
            pltpu.VMEM((2,) + half, f32),
            pltpu.SemaphoreType.DMA((2,)),
            pltpu.SemaphoreType.DMA((2, chips)),
            pltpu.SemaphoreType.DMA((2, chips)),
            pltpu.SemaphoreType.DMA((2,)),
        ],
        compiler_params=pltpu.CompilerParams(collective_id=0 if whole else 2, has_side_effects=True),
        name="device_sum" if whole else "far_sum",
    )(value.reshape((2,) + half) if whole else value)
    return out.reshape(height, width)


def gram_kernel(early_tiles, s_ref, out_ref, raw_ref, cross_ref):
    step = pl.program_id(0)
    value = s_ref[...]
    high = value.astype(jnp.bfloat16)
    rest = value - high.astype(jnp.float32)
    mid = rest.astype(jnp.bfloat16)
    low = (rest - mid.astype(jnp.float32)).astype(jnp.bfloat16)
    rows = ((0,), (0,))
    square = dot(high, high, rows, None) + dot(mid, mid, rows, None)
    cross = dot(high, mid, rows, None) + dot(high, low, rows, None)

    @pl.when(step == 0)
    def _():
        out_ref[...] = square
        cross_ref[...] = cross

    @pl.when(step > 0)
    def _():
        out_ref[...] += square
        cross_ref[...] += cross

    @pl.when(step < early_tiles)
    def _():
        raw_ref[...] = value

    @pl.when(step == pl.num_programs(0) - 1)
    def _():
        cross = cross_ref[...]
        out_ref[...] += cross + cross.T


def gram_of(snapshots, early, tile=512):
    height, width = snapshots.shape
    early_tiles = early // tile
    return pl.pallas_call(
        functools.partial(gram_kernel, early_tiles),
        grid=(height // tile,),
        in_specs=[pl.BlockSpec((tile, width), lambda i: (i, 0))],
        out_specs=(
            pl.BlockSpec((width, width), lambda i: (0, 0)),
            pl.BlockSpec((tile, width), lambda i: (jnp.minimum(i, early_tiles - 1), 0)),
        ),
        out_shape=(
            jax.ShapeDtypeStruct((width, width), jnp.float32),
            jax.ShapeDtypeStruct((early, width), jnp.float32),
        ),
        scratch_shapes=[pltpu.VMEM((width, width), jnp.float32)],
        compiler_params=pltpu.CompilerParams(vmem_limit_bytes=16 * 2**20),
        name="gram",
    )(snapshots)


def project_kernel(per_step, columns_ref, blocks_ref, basis_ref, *refs):
    *parts, out_ref, window_ref, sems = refs
    step = pl.program_id(0)
    stored, block_len = blocks_ref.shape[1], blocks_ref.shape[2]

    @pl.when(step == 0)
    def _():
        out_ref[...] = jnp.zeros_like(out_ref)
        copies, at = [], 0
        for index, part in enumerate(parts):
            size = part.shape[0]
            copies.append(pltpu.make_async_copy(part, window_ref.at[pl.ds(at, size)], sems.at[index]))
            at += size
        for copy in copies:
            copy.start()
        for copy in copies:
            copy.wait()

    images = []
    for r in range(per_step):
        picked = []
        for j in range(stored):
            at = columns_ref[step * per_step + r, j] * block_len
            picked.append(window_ref[pl.ds(pl.multiple_of(at, block_len), block_len), :])
        left = jnp.concatenate([blocks_ref[r, j] for j in range(stored)], axis=1)
        right = jnp.concatenate(picked, axis=0)
        images.append(jnp.dot(left, right, preferred_element_type=jnp.float32))
    image = jnp.concatenate(images, axis=0)
    image_high, image_low = split(image)
    basis_high, basis_low = split(basis_ref[...])
    rows = ((0,), (0,))
    term = dot(basis_high, image_high, rows, None)
    term = term + dot(basis_high, image_low, rows, None)
    term = term + dot(basis_low, image_high, rows, None)
    out_ref[...] += term


def project(columns, blocks, basis, parts):
    block_rows, stored, block_len, _ = blocks.shape
    width = basis.shape[1]
    per_step = 2
    depth = sum(part.shape[0] for part in parts)
    grid_spec = pltpu.PrefetchScalarGridSpec(
        num_scalar_prefetch=1,
        grid=(block_rows // per_step,),
        in_specs=[
            pl.BlockSpec((per_step, stored, block_len, block_len), lambda i, c: (i, 0, 0, 0)),
            pl.BlockSpec((per_step * block_len, width), lambda i, c: (i, 0)),
        ] + [pl.BlockSpec(memory_space=pl.ANY)] * len(parts),
        out_specs=pl.BlockSpec((width, width), lambda i, c: (0, 0)),
        scratch_shapes=[
            pltpu.VMEM((depth, width), jnp.bfloat16),
            pltpu.SemaphoreType.DMA((len(parts),)),
        ],
    )
    return pl.pallas_call(
        functools.partial(project_kernel, per_step),
        grid_spec=grid_spec,
        out_shape=jax.ShapeDtypeStruct((width, width), jnp.float32),
        compiler_params=pltpu.CompilerParams(vmem_limit_bytes=40 * 2**20),
        name="project",
    )(columns, blocks, basis, *parts)


def ring(value, axis):
    size = lax.axis_size(axis)
    for shift in range(1, size):
        yield lax.ppermute(value, axis, [((d + shift) % size, d) for d in range(size)])


def local(snapshots, blocks, columns):
    axes = ("rows", "grp")
    height = snapshots.shape[0]
    early = height // 4
    gram, raw = gram_of(snapshots, early)
    near = near_sum(gram, axes, lax.axis_size("rows") // 2)
    near, raw = lax.optimization_barrier((near, raw))
    raws = list(ring(raw, "grp"))
    factor, inverse = factorize(device_sum(near, axes, whole=False))
    cuts = (early, early + height // 4, height)
    pieces, lates = [], []
    for start, stop in zip(cuts[:-1], cuts[1:]):
        pieces.append(dot(snapshots[start:stop], inverse))
        lates.append(list(ring(pieces[-1].astype(jnp.bfloat16), "grp")))
    basis = jnp.concatenate([dot(snapshots[:early], inverse)] + pieces, axis=0)
    basis_half = basis.astype(jnp.bfloat16)
    parts = [basis_half]
    for index, raw in enumerate(raws):
        parts += [dot(raw, inverse).astype(jnp.bfloat16)] + [late[index] for late in lates]
    block_rows = blocks.shape[0]
    size = lax.axis_size("grp")
    turned = lax.rem(columns + (size - lax.axis_index("grp")) * block_rows, size * block_rows)
    projected = device_sum(project(turned, blocks, basis, parts), axes)
    total_rows = height * lax.axis_size(axes)
    return projected, factor / math.sqrt(total_rows)


def solution(mesh):
    return jax.shard_map(
        local,
        mesh=mesh,
        in_specs=(
            P(("rows", "grp"), None),
            P(("rows", "grp"), None, None, None),
            P(("rows", "grp"), None),
        ),
        out_specs=(P(), P()),
        check_vma=False,
    )
```

```python
import functools
import math

import jax
import jax.numpy as jnp
from jax import lax
from jax.experimental import pallas as pl
from jax.experimental.pallas import tpu as pltpu
from jax.sharding import PartitionSpec as P

HIGHEST = lax.Precision.HIGHEST
LANES = 128
SUB = 8
MESH = pl.DeviceIdType.MESH


def dot(left, right, dims=((1,), (0,)), precision=HIGHEST):
    return lax.dot_general(
        left, right, (dims, ((), ())), precision=precision, preferred_element_type=jnp.float32
    )


def across(value, lane, shape):
    return jnp.broadcast_to(value[..., lane : lane + 1], shape)


def eliminate(head, tail):
    tiles = head.shape[0]
    one = (SUB, LANES)
    for tile in range(tiles):
        base = tile * SUB
        rows_h = [jnp.broadcast_to(head[tile, k : k + 1, :], one) for k in range(SUB)]
        rows_t = [jnp.broadcast_to(tail[tile, k : k + 1, :], one) for k in range(SUB)]
        d = {}
        for k in range(SUB):
            for i in range(k, SUB):
                d[k, i] = across(rows_h[k], base + i, one)
        later = tiles - tile - 1
        if later:
            rest_h = head[tile + 1 :]
            rest_t = tail[tile + 1 :]
            low = [across(rest_h, base + k, (later, SUB, LANES)) for k in range(SUB)]
        for k in range(SUB):
            scale = lax.rsqrt(d[k, k])
            for i in range(k + 1, SUB):
                d[k, i] = d[k, i] * scale
            rows_h[k] = rows_h[k] * scale
            rows_t[k] = rows_t[k] * scale
            for i in range(k + 1, SUB):
                for m in range(i, SUB):
                    d[i, m] = d[i, m] - d[k, i] * d[k, m]
                rows_h[i] = rows_h[i] - d[k, i] * rows_h[k]
                rows_t[i] = rows_t[i] - d[k, i] * rows_t[k]
            if later:
                low[k] = low[k] * scale[None]
                for m in range(k + 1, SUB):
                    low[m] = low[m] - low[k] * d[k, m][None]
                rest_h = rest_h - low[k] * rows_h[k][None]
                rest_t = rest_t - low[k] * rows_t[k][None]
            head[tile, k : k + 1, :] = rows_h[k][:1]
            tail[tile, k : k + 1, :] = rows_t[k][:1]
        if later:
            head[tile + 1 :] = rest_h
            tail[tile + 1 :] = rest_t


def factor_kernel(gram_ref, factor_ref, inverse_ref, head, tail):
    size = gram_ref.shape[0]
    n = LANES
    row = lax.broadcasted_iota(jnp.int32, (n, n), 0)
    col = lax.broadcasted_iota(jnp.int32, (n, n), 1)
    eye = jnp.where(row == col, 1.0, 0.0).astype(jnp.float32)
    tiles = (n // SUB, SUB, n)
    count = size // n

    for b in range(count):
        here = slice(b * n, (b + 1) * n)
        square = gram_ref[here, here]
        for a in range(b):
            above = factor_ref[a * n : (a + 1) * n, here]
            square = square - dot(above, above, ((0,), (0,)))
        head[...] = square.reshape(tiles)
        tail[...] = eye.reshape(tiles)
        eliminate(head, tail)
        lower = jnp.where(row >= col, tail[...].reshape(n, n), 0.0)
        factor_ref[here, here] = jnp.where(row <= col, head[...].reshape(n, n), 0.0)
        upper = lower.T
        inverse_ref[here, here] = upper
        for c in range(b + 1, count):
            there = slice(c * n, (c + 1) * n)
            rest = gram_ref[here, there]
            for a in range(b):
                span = slice(a * n, (a + 1) * n)
                rest = rest - dot(factor_ref[span, here], factor_ref[span, there], ((0,), (0,)))
            factor_ref[here, there] = dot(lower, rest)
            factor_ref[there, here] = jnp.zeros((n, n), jnp.float32)
            inverse_ref[there, here] = jnp.zeros((n, n), jnp.float32)
        for a in range(b):
            span = slice(a * n, (a + 1) * n)
            total = jnp.zeros((n, n), jnp.float32)
            for m in range(a, b):
                mid = slice(m * n, (m + 1) * n)
                total = total + dot(inverse_ref[span, mid], factor_ref[mid, here])
            inverse_ref[span, here] = -dot(total, upper)


def factorize(gram):
    size = gram.shape[0]
    square = jax.ShapeDtypeStruct((size, size), jnp.float32)
    return pl.pallas_call(
        factor_kernel,
        out_shape=(square, square),
        in_specs=[pl.BlockSpec(memory_space=pltpu.VMEM)],
        out_specs=(pl.BlockSpec(memory_space=pltpu.VMEM),) * 2,
        scratch_shapes=[pltpu.VMEM((LANES // SUB, SUB, LANES), jnp.float32)] * 2,
        compiler_params=pltpu.CompilerParams(vmem_limit_bytes=16 * 2**20),
        name="factorize",
    )(gram)


def split(value):
    high = value.astype(jnp.bfloat16)
    return high, (value - high.astype(jnp.float32)).astype(jnp.bfloat16)


def mate_of(axes):
    row = lax.axis_index(axes[0])
    return {axes[0]: row + 1 - 2 * lax.rem(row, 2), axes[1]: lax.axis_index(axes[1])}


def greet(barrier, where):
    pl.semaphore_signal(barrier, inc=1, device_id=where, device_id_type=MESH)


def exchange(source, target, sems, where):
    return pltpu.make_async_remote_copy(
        src_ref=source, dst_ref=target, send_sem=sems.at[0], recv_sem=sems.at[1],
        device_id=where, device_id_type=MESH)


def near_kernel(axes, grps, x_ref, out_ref, pair, own, others, pair_sems, grp_sems):
    me_row, me_grp = lax.axis_index(axes[0]), lax.axis_index(axes[1])
    core = lax.rem(me_row, 2)
    mate = mate_of(axes)
    friends = [{axes[0]: me_row, axes[1]: lax.rem(me_grp + shift, grps)} for shift in range(1, grps)]
    barrier = pltpu.get_barrier_semaphore()
    for where in [mate] + friends:
        greet(barrier, where)
    pl.semaphore_wait(barrier, grps)
    first = exchange(x_ref.at[1 - core], pair, pair_sems, mate)
    first.start()
    first.wait()
    own[...] = x_ref[core] + pair[...]
    copies = [exchange(own, others.at[i], grp_sems.at[i], where) for i, where in enumerate(friends)]
    for copy in copies:
        copy.start()
    total = own[...]
    for i, copy in enumerate(copies):
        copy.wait()
        total = total + others[i]
    out_ref[...] = total


def near_sum(value, axes, chips):
    height, width = value.shape
    grps = lax.axis_size(axes[1])
    half = (chips, height // (2 * chips), width)
    f32 = jnp.float32
    return pl.pallas_call(
        functools.partial(near_kernel, axes, grps),
        out_shape=jax.ShapeDtypeStruct(half, f32),
        in_specs=[pl.BlockSpec(memory_space=pltpu.VMEM)],
        out_specs=pl.BlockSpec(memory_space=pltpu.VMEM),
        scratch_shapes=[
            pltpu.VMEM(half, f32),
            pltpu.VMEM(half, f32),
            pltpu.VMEM((grps - 1,) + half, f32),
            pltpu.SemaphoreType.DMA((2,)),
            pltpu.SemaphoreType.DMA((grps - 1, 2)),
        ],
        compiler_params=pltpu.CompilerParams(collective_id=1, has_side_effects=True),
        name="near_sum",
    )(value.reshape((2,) + half))


def sum_kernel(axes, grps, x_ref, out_ref, pair, own, slots, held, pair_sems, scatter_sems, gather_sems, last_sems):
    rows_axis, grp_axis = axes
    chips = own.shape[0]
    me_row, me_grp = lax.axis_index(rows_axis), lax.axis_index(grp_axis)
    core = lax.rem(me_row, 2)
    mate = mate_of(axes)
    whole = grps > 1
    me = (me_row // 2) * grps + me_grp if whole else me_row // 2

    def chip(offset):
        other = lax.rem(me + offset, chips)
        if whole:
            return other, {rows_axis: (other // grps) * 2 + core, grp_axis: lax.rem(other, grps)}
        return other, {rows_axis: other * 2 + core, grp_axis: me_grp}

    barrier = pltpu.get_barrier_semaphore()
    greet(barrier, mate)

    def greet_chip(offset, carry):
        greet(barrier, chip(offset)[1])
        return carry

    lax.fori_loop(1, chips, greet_chip, 0, unroll=chips <= 16)
    pl.semaphore_wait(barrier, chips)

    if whole:
        first = exchange(x_ref.at[1 - core], pair, pair_sems, mate)
        first.start()
        first.wait()
        own[...] = x_ref[core] + pair[...]
    else:
        own[...] = x_ref[...]

    def scatter(offset):
        other, where = chip(offset)
        return pltpu.make_async_remote_copy(
            src_ref=own.at[other], dst_ref=slots.at[offset],
            send_sem=scatter_sems.at[0, offset], recv_sem=scatter_sems.at[1, offset],
            device_id=where, device_id_type=MESH)

    def gather(offset):
        _, where = chip(offset)
        return pltpu.make_async_remote_copy(
            src_ref=held.at[core, me], dst_ref=held.at[core, me],
            send_sem=gather_sems.at[0, offset], recv_sem=gather_sems.at[1, offset],
            device_id=where, device_id_type=MESH)

    def each(make, act):
        def body(offset, carry):
            getattr(make(offset), act)()
            return carry
        lax.fori_loop(1, chips, body, 0, unroll=chips <= 16)

    each(scatter, "start")
    slots[0] = own[me]
    each(scatter, "wait_recv")
    held[core, me] = jnp.sum(slots[...], axis=0)
    each(gather, "start")
    each(scatter, "wait_send")
    each(gather, "wait_recv")
    last = exchange(held.at[core], held.at[core], last_sems, mate)
    last.start()
    each(gather, "wait_send")
    last.wait()
    out_ref[...] = held[...]


def device_sum(value, axes, whole=True):
    grps = lax.axis_size(axes[1]) if whole else 1
    chips = lax.axis_size(axes[0]) // 2 * grps
    height, width = (value.shape[0], value.shape[1]) if whole else (2 * chips * value.shape[1], value.shape[2])
    half = (chips, height // (2 * chips), width)
    f32 = jnp.float32
    out = pl.pallas_call(
        functools.partial(sum_kernel, axes, grps),
        out_shape=jax.ShapeDtypeStruct((2,) + half, f32),
        in_specs=[pl.BlockSpec(memory_space=pltpu.VMEM)],
        out_specs=pl.BlockSpec(memory_space=pltpu.VMEM),
        scratch_shapes=[
            pltpu.VMEM(half, f32),
            pltpu.VMEM(half, f32),
            pltpu.VMEM(half, f32),
            pltpu.VMEM((2,) + half, f32),
            pltpu.SemaphoreType.DMA((2,)),
            pltpu.SemaphoreType.DMA((2, chips)),
            pltpu.SemaphoreType.DMA((2, chips)),
            pltpu.SemaphoreType.DMA((2,)),
        ],
        compiler_params=pltpu.CompilerParams(collective_id=0 if whole else 2, has_side_effects=True),
        name="device_sum" if whole else "far_sum",
    )(value.reshape((2,) + half) if whole else value)
    return out.reshape(height, width)


def gram_kernel(early_tiles, s_ref, out_ref, raw_ref, cross_ref):
    step = pl.program_id(0)
    value = s_ref[...]
    high = value.astype(jnp.bfloat16)
    rest = value - high.astype(jnp.float32)
    mid = rest.astype(jnp.bfloat16)
    low = (rest - mid.astype(jnp.float32)).astype(jnp.bfloat16)
    rows = ((0,), (0,))
    square = dot(high, high, rows, None) + dot(mid, mid, rows, None)
    cross = dot(high, mid, rows, None) + dot(high, low, rows, None)

    @pl.when(step == 0)
    def _():
        out_ref[...] = square
        cross_ref[...] = cross

    @pl.when(step > 0)
    def _():
        out_ref[...] += square
        cross_ref[...] += cross

    @pl.when(step < early_tiles)
    def _():
        raw_ref[...] = value

    @pl.when(step == pl.num_programs(0) - 1)
    def _():
        cross = cross_ref[...]
        out_ref[...] += cross + cross.T


def gram_of(snapshots, early, tile=512):
    height, width = snapshots.shape
    early_tiles = early // tile
    return pl.pallas_call(
        functools.partial(gram_kernel, early_tiles),
        grid=(height // tile,),
        in_specs=[pl.BlockSpec((tile, width), lambda i: (i, 0))],
        out_specs=(
            pl.BlockSpec((width, width), lambda i: (0, 0)),
            pl.BlockSpec((tile, width), lambda i: (jnp.minimum(i, early_tiles - 1), 0)),
        ),
        out_shape=(
            jax.ShapeDtypeStruct((width, width), jnp.float32),
            jax.ShapeDtypeStruct((early, width), jnp.float32),
        ),
        scratch_shapes=[pltpu.VMEM((width, width), jnp.float32)],
        compiler_params=pltpu.CompilerParams(vmem_limit_bytes=16 * 2**20),
        name="gram",
    )(snapshots)


def split3(value):
    high = value.astype(jnp.bfloat16)
    rest = value - high.astype(jnp.float32)
    return (high,) + split(rest)


def basis_kernel(s_ref, inverse_ref, *outs):
    sh, sm, sl = split3(s_ref[...])
    wh, wm, wl = split3(inverse_ref[...])
    plain = ((1,), (0,))
    small = dot(sl, wh, plain, None) + dot(sm, wm, plain, None) + dot(sh, wl, plain, None)
    value = small + (dot(sm, wh, plain, None) + dot(sh, wm, plain, None)) + dot(sh, wh, plain, None)
    for out in outs:
        out[...] = value.astype(out.dtype)


def basis_of(rows, inverse, start, stop, dtypes, tile=512):
    width = rows.shape[1]
    first = start // tile
    spec = pl.BlockSpec((tile, width), lambda i: (i, 0))
    return pl.pallas_call(
        basis_kernel,
        grid=((stop - start) // tile,),
        in_specs=[
            pl.BlockSpec((tile, width), lambda i: (i + first, 0)),
            pl.BlockSpec((width, width), lambda i: (0, 0)),
        ],
        out_specs=tuple(spec for _ in dtypes),
        out_shape=tuple(jax.ShapeDtypeStruct((stop - start, width), dtype) for dtype in dtypes),
        compiler_params=pltpu.CompilerParams(vmem_limit_bytes=16 * 2**20),
        cost_estimate=pl.CostEstimate(
            flops=12 * (stop - start) * width * width,
            bytes_accessed=8 * (stop - start) * width, transcendentals=0),
        name="basis",
    )(rows, inverse)


def fill(window_ref, sems, parts, block_len):
    copies, at = [], 0
    for index, part in enumerate(parts):
        size = part.shape[0]
        copies.append(pltpu.make_async_copy(part, window_ref.at[pl.ds(at, size)], sems.at[index]))
        at += size
    for copy in copies:
        copy.start()
    window_ref[at : at + block_len] = jnp.zeros((block_len, window_ref.shape[1]), window_ref.dtype)
    for copy in copies:
        copy.wait()


def project_kernel(per_step, slots, edges, n_parts, *refs):
    places_ref, picks_ref, counts_ref, blocks_ref = refs[:4]
    basis_refs = refs[4 : 4 + len(edges)]
    before_ref = refs[4 + len(edges)]
    parts = refs[5 + len(edges) : 5 + len(edges) + n_parts]
    out_ref, window_ref, image_ref, sems = refs[5 + len(edges) + n_parts :]
    step = pl.program_id(0)
    stored, block_len = blocks_ref.shape[1], blocks_ref.shape[2]

    @pl.when(step == 0)
    def _():
        out_ref[...] = before_ref[...]
        fill(window_ref, sems, parts, block_len)

    def product(r, first):
        row = step * per_step + r
        lefts, rights = [], []
        for slot in range(first, first + slots):
            at = places_ref[row, slot] * block_len
            rights.append(window_ref[pl.ds(pl.multiple_of(at, block_len), block_len), :])
            lefts.append(blocks_ref[r, slot if slots == stored else picks_ref[row, slot]])
        left = jnp.concatenate(lefts, axis=1)
        right = jnp.concatenate(rights, axis=0)
        return jnp.dot(left, right, preferred_element_type=jnp.float32)

    for r in range(per_step):
        image_ref[r * block_len : (r + 1) * block_len] = product(r, 0)
    for first in range(slots, stored, slots):
        for r in range(per_step):

            @pl.when(counts_ref[step * per_step + r, 0] > first)
            def _():
                image_ref[r * block_len : (r + 1) * block_len] += product(r, first)

    value = basis_refs[-1][...]
    for edge, ref in reversed(list(zip(edges[1:], basis_refs[:-1]))):
        value = jnp.where(step < edge, ref[...], value)
    image_high, image_low = split(image_ref[...])
    basis_high, basis_low = split(value)
    rows = ((0,), (0,))
    term = dot(basis_high, image_high, rows, None)
    term = term + dot(basis_high, image_low, rows, None)
    term = term + dot(basis_low, image_high, rows, None)
    out_ref[...] += term


def project(places, picks, counts, blocks, basis, before, parts, slots, per_step=2):
    block_rows, stored, block_len, _ = blocks.shape
    width = before.shape[1]
    depth = sum(part.shape[0] for part in parts) + block_len
    tall = per_step * block_len
    edges, specs, at = [], [], 0
    for part in basis:
        steps = part.shape[0] // tall
        edges.append(at)
        specs.append(pl.BlockSpec(
            (tall, width),
            functools.partial(lambda at, steps, i, *_: (jnp.clip(i - at, 0, steps - 1), 0), at, steps)))
        at += steps
    grid_spec = pltpu.PrefetchScalarGridSpec(
        num_scalar_prefetch=3,
        grid=(block_rows // per_step,),
        in_specs=[pl.BlockSpec((per_step, stored, block_len, block_len), lambda i, *_: (i, 0, 0, 0))]
        + specs
        + [pl.BlockSpec((width, width), lambda i, *_: (0, 0))]
        + [pl.BlockSpec(memory_space=pl.ANY)] * len(parts),
        out_specs=pl.BlockSpec((width, width), lambda i, *_: (0, 0)),
        scratch_shapes=[
            pltpu.VMEM((depth, width), jnp.bfloat16),
            pltpu.VMEM((tall, width), jnp.float32),
            pltpu.SemaphoreType.DMA((len(parts),)),
        ],
    )
    return pl.pallas_call(
        functools.partial(project_kernel, per_step, slots, tuple(edges), len(parts)),
        grid_spec=grid_spec,
        out_shape=jax.ShapeDtypeStruct((width, width), jnp.float32),
        compiler_params=pltpu.CompilerParams(vmem_limit_bytes=44 * 2**20),
        cost_estimate=pl.CostEstimate(
            flops=2 * block_rows * slots * block_len * block_len * width,
            bytes_accessed=blocks.size * 2, transcendentals=0),
        name="project",
    )(places, picks, counts, blocks, *basis, before, *parts)


def ring(value, axis):
    size = lax.axis_size(axis)
    for shift in range(1, size):
        yield lax.ppermute(value, axis, [((d + shift) % size, d) for d in range(size)])


def plan_kernel(size, early, columns_ref, places_ref, picks_ref, late_places_ref, counts_ref):
    block_rows, stored = columns_ref.shape
    turned = lax.rem(columns_ref[...] + (size - lax.axis_index("grp")) * block_rows, size * block_rows)
    slab, row = turned // block_rows, lax.rem(turned, block_rows)
    wanted = jnp.where((slab == 0) | (row < early), 0, 1)
    near = jnp.where(slab == 0, row, block_rows + (slab - 1) * early + row)
    places_ref[...] = jnp.where(wanted == 1, block_rows + (size - 1) * early, near)
    late = (slab - 1) * (block_rows - early) + row - early
    slot = lax.broadcasted_iota(jnp.int32, (block_rows, stored), 1)
    rank = jnp.zeros((block_rows, stored), jnp.int32)
    picks = jnp.zeros((block_rows, stored), jnp.int32)
    late_places = jnp.full((block_rows, stored), (size - 1) * (block_rows - early), jnp.int32)
    for j in range(stored):
        needs = across(wanted, j, rank.shape)
        here = (needs == 1) & (rank == slot)
        picks = jnp.where(here, j, picks)
        late_places = jnp.where(here, across(late, j, rank.shape), late_places)
        rank = rank + needs
    picks_ref[...] = picks
    late_places_ref[...] = late_places
    counts_ref[...] = rank


def plan(columns, size, early):
    return pl.pallas_call(
        functools.partial(plan_kernel, size, early),
        out_shape=(jax.ShapeDtypeStruct(columns.shape, jnp.int32),) * 4,
        name="plan",
    )(columns)


def local(snapshots, blocks, columns):
    axes = ("rows", "grp")
    height, width = snapshots.shape
    block_len, stored = blocks.shape[2], blocks.shape[1]
    size = lax.axis_size("grp")
    early = height * 3 // 8
    half, full = jnp.bfloat16, jnp.float32
    places, picks, late_places, counts = plan(columns, size, early // block_len)
    gram, raw = gram_of(snapshots, early)
    near = near_sum(gram, axes, lax.axis_size("rows") // 2)
    near, raw = lax.optimization_barrier((near, raw))
    raws = list(ring(raw, "grp"))
    factor, inverse = factorize(device_sum(near, axes, whole=False))
    cuts = (early, early + height // 8, height)
    pieces, halves, lates = [], [], []
    for start, stop in zip(cuts[:-1], cuts[1:]):
        piece, piece_half = basis_of(snapshots, inverse, start, stop, (full, half))
        pieces.append(piece)
        halves.append(piece_half)
        lates.append(list(ring(piece_half, "grp")))
        inverse, _ = lax.optimization_barrier((inverse, piece_half))
    piece, piece_half = basis_of(snapshots, inverse, 0, early, (full, half))
    basis = [piece] + pieces
    first = [piece_half] + halves + [basis_of(raw, inverse, 0, early, (half,))[0] for raw in raws]
    second = [late[index] for index in range(size - 1) for late in lates]
    zero = jnp.zeros((width, width), full)
    partial_terms = project(places, picks, counts, blocks, basis, zero, first, stored)
    partial_terms = project(late_places, picks, counts, blocks, basis, partial_terms, second, stored // 2)
    projected = device_sum(partial_terms, axes)
    total_rows = height * lax.axis_size(axes)
    return projected, factor / math.sqrt(total_rows)


def solution(mesh):
    return jax.shard_map(
        local,
        mesh=mesh,
        in_specs=(
            P(("rows", "grp"), None),
            P(("rows", "grp"), None, None, None),
            P(("rows", "grp"), None),
        ),
        out_specs=(P(), P()),
        check_vma=False,
    )
```

```python
import functools
import math

import jax
import jax.numpy as jnp
from jax import lax
from jax.experimental import pallas as pl
from jax.experimental.pallas import tpu as pltpu
from jax.sharding import PartitionSpec as P

HIGHEST = lax.Precision.HIGHEST
LANES = 128
SUB = 8
MESH = pl.DeviceIdType.MESH


def dot(left, right, dims=((1,), (0,)), precision=HIGHEST):
    return lax.dot_general(
        left, right, (dims, ((), ())), precision=precision, preferred_element_type=jnp.float32
    )


def across(value, lane, shape):
    return jnp.broadcast_to(value[..., lane : lane + 1], shape)


def eliminate(head, tail):
    tiles = head.shape[0]
    one = (SUB, LANES)
    for tile in range(tiles):
        base = tile * SUB
        rows_h = [jnp.broadcast_to(head[tile, k : k + 1, :], one) for k in range(SUB)]
        rows_t = [jnp.broadcast_to(tail[tile, k : k + 1, :], one) for k in range(SUB)]
        d = {}
        for k in range(SUB):
            for i in range(k, SUB):
                d[k, i] = across(rows_h[k], base + i, one)
        later = tiles - tile - 1
        if later:
            rest_h = head[tile + 1 :]
            rest_t = tail[tile + 1 :]
            low = [across(rest_h, base + k, (later, SUB, LANES)) for k in range(SUB)]
        for k in range(SUB):
            scale = lax.rsqrt(d[k, k])
            for i in range(k + 1, SUB):
                d[k, i] = d[k, i] * scale
            rows_h[k] = rows_h[k] * scale
            rows_t[k] = rows_t[k] * scale
            for i in range(k + 1, SUB):
                for m in range(i, SUB):
                    d[i, m] = d[i, m] - d[k, i] * d[k, m]
                rows_h[i] = rows_h[i] - d[k, i] * rows_h[k]
                rows_t[i] = rows_t[i] - d[k, i] * rows_t[k]
            if later:
                low[k] = low[k] * scale[None]
                for m in range(k + 1, SUB):
                    low[m] = low[m] - low[k] * d[k, m][None]
                rest_h = rest_h - low[k] * rows_h[k][None]
                rest_t = rest_t - low[k] * rows_t[k][None]
            head[tile, k : k + 1, :] = rows_h[k][:1]
            tail[tile, k : k + 1, :] = rows_t[k][:1]
        if later:
            head[tile + 1 :] = rest_h
            tail[tile + 1 :] = rest_t


def factor_kernel(gram_ref, factor_ref, inverse_ref, head, tail):
    size = gram_ref.shape[0]
    n = LANES
    row = lax.broadcasted_iota(jnp.int32, (n, n), 0)
    col = lax.broadcasted_iota(jnp.int32, (n, n), 1)
    eye = jnp.where(row == col, 1.0, 0.0).astype(jnp.float32)
    tiles = (n // SUB, SUB, n)
    count = size // n

    for b in range(count):
        here = slice(b * n, (b + 1) * n)
        square = gram_ref[here, here]
        for a in range(b):
            above = factor_ref[a * n : (a + 1) * n, here]
            square = square - dot(above, above, ((0,), (0,)))
        head[...] = square.reshape(tiles)
        tail[...] = eye.reshape(tiles)
        eliminate(head, tail)
        lower = jnp.where(row >= col, tail[...].reshape(n, n), 0.0)
        factor_ref[here, here] = jnp.where(row <= col, head[...].reshape(n, n), 0.0)
        upper = lower.T
        inverse_ref[here, here] = upper
        for c in range(b + 1, count):
            there = slice(c * n, (c + 1) * n)
            rest = gram_ref[here, there]
            for a in range(b):
                span = slice(a * n, (a + 1) * n)
                rest = rest - dot(factor_ref[span, here], factor_ref[span, there], ((0,), (0,)))
            factor_ref[here, there] = dot(lower, rest)
            factor_ref[there, here] = jnp.zeros((n, n), jnp.float32)
            inverse_ref[there, here] = jnp.zeros((n, n), jnp.float32)
        for a in range(b):
            span = slice(a * n, (a + 1) * n)
            total = jnp.zeros((n, n), jnp.float32)
            for m in range(a, b):
                mid = slice(m * n, (m + 1) * n)
                total = total + dot(inverse_ref[span, mid], factor_ref[mid, here])
            inverse_ref[span, here] = -dot(total, upper)


def factorize(gram):
    size = gram.shape[0]
    square = jax.ShapeDtypeStruct((size, size), jnp.float32)
    return pl.pallas_call(
        factor_kernel,
        out_shape=(square, square),
        in_specs=[pl.BlockSpec(memory_space=pltpu.VMEM)],
        out_specs=(pl.BlockSpec(memory_space=pltpu.VMEM),) * 2,
        scratch_shapes=[pltpu.VMEM((LANES // SUB, SUB, LANES), jnp.float32)] * 2,
        compiler_params=pltpu.CompilerParams(vmem_limit_bytes=16 * 2**20),
        name="factorize",
    )(gram)


def split(value):
    high = value.astype(jnp.bfloat16)
    return high, (value - high.astype(jnp.float32)).astype(jnp.bfloat16)


def mate_of(axes):
    row = lax.axis_index(axes[0])
    return {axes[0]: row + 1 - 2 * lax.rem(row, 2), axes[1]: lax.axis_index(axes[1])}


def greet(barrier, where):
    pl.semaphore_signal(barrier, inc=1, device_id=where, device_id_type=MESH)


def exchange(source, target, sems, where):
    return pltpu.make_async_remote_copy(
        src_ref=source, dst_ref=target, send_sem=sems.at[0], recv_sem=sems.at[1],
        device_id=where, device_id_type=MESH)


def near_kernel(axes, grps, x_ref, out_ref, pair, own, others, pair_sems, grp_sems):
    me_row, me_grp = lax.axis_index(axes[0]), lax.axis_index(axes[1])
    core = lax.rem(me_row, 2)
    mate = mate_of(axes)
    friends = [{axes[0]: me_row, axes[1]: lax.rem(me_grp + shift, grps)} for shift in range(1, grps)]
    barrier = pltpu.get_barrier_semaphore()
    for where in [mate] + friends:
        greet(barrier, where)
    pl.semaphore_wait(barrier, grps)
    first = exchange(x_ref.at[1 - core], pair, pair_sems, mate)
    first.start()
    first.wait()
    own[...] = x_ref[core] + pair[...]
    copies = [exchange(own, others.at[i], grp_sems.at[i], where) for i, where in enumerate(friends)]
    for copy in copies:
        copy.start()
    total = own[...]
    for i, copy in enumerate(copies):
        copy.wait()
        total = total + others[i]
    out_ref[...] = total


def near_sum(value, axes, chips):
    height, width = value.shape
    grps = lax.axis_size(axes[1])
    half = (chips, height // (2 * chips), width)
    f32 = jnp.float32
    return pl.pallas_call(
        functools.partial(near_kernel, axes, grps),
        out_shape=jax.ShapeDtypeStruct(half, f32),
        in_specs=[pl.BlockSpec(memory_space=pltpu.VMEM)],
        out_specs=pl.BlockSpec(memory_space=pltpu.VMEM),
        scratch_shapes=[
            pltpu.VMEM(half, f32),
            pltpu.VMEM(half, f32),
            pltpu.VMEM((grps - 1,) + half, f32),
            pltpu.SemaphoreType.DMA((2,)),
            pltpu.SemaphoreType.DMA((grps - 1, 2)),
        ],
        compiler_params=pltpu.CompilerParams(collective_id=1, has_side_effects=True),
        name="near_sum",
    )(value.reshape((2,) + half))


def sum_kernel(axes, grps, x_ref, out_ref, pair, own, slots, held, pair_sems, scatter_sems, gather_sems, last_sems):
    rows_axis, grp_axis = axes
    chips = own.shape[0]
    me_row, me_grp = lax.axis_index(rows_axis), lax.axis_index(grp_axis)
    core = lax.rem(me_row, 2)
    mate = mate_of(axes)
    whole = grps > 1
    me = (me_row // 2) * grps + me_grp if whole else me_row // 2

    def chip(offset):
        other = lax.rem(me + offset, chips)
        if whole:
            return other, {rows_axis: (other // grps) * 2 + core, grp_axis: lax.rem(other, grps)}
        return other, {rows_axis: other * 2 + core, grp_axis: me_grp}

    barrier = pltpu.get_barrier_semaphore()
    greet(barrier, mate)

    def greet_chip(offset, carry):
        greet(barrier, chip(offset)[1])
        return carry

    lax.fori_loop(1, chips, greet_chip, 0, unroll=chips <= 16)
    pl.semaphore_wait(barrier, chips)

    if whole:
        first = exchange(x_ref.at[1 - core], pair, pair_sems, mate)
        first.start()
        first.wait()
        own[...] = x_ref[core] + pair[...]
    else:
        own[...] = x_ref[...]

    def scatter(offset):
        other, where = chip(offset)
        return pltpu.make_async_remote_copy(
            src_ref=own.at[other], dst_ref=slots.at[offset],
            send_sem=scatter_sems.at[0, offset], recv_sem=scatter_sems.at[1, offset],
            device_id=where, device_id_type=MESH)

    def gather(offset):
        _, where = chip(offset)
        return pltpu.make_async_remote_copy(
            src_ref=held.at[core, me], dst_ref=held.at[core, me],
            send_sem=gather_sems.at[0, offset], recv_sem=gather_sems.at[1, offset],
            device_id=where, device_id_type=MESH)

    def each(make, act):
        def body(offset, carry):
            getattr(make(offset), act)()
            return carry
        lax.fori_loop(1, chips, body, 0, unroll=chips <= 16)

    each(scatter, "start")
    slots[0] = own[me]
    each(scatter, "wait_recv")
    held[core, me] = jnp.sum(slots[...], axis=0)
    each(gather, "start")
    each(scatter, "wait_send")
    each(gather, "wait_recv")
    last = exchange(held.at[core], held.at[core], last_sems, mate)
    last.start()
    each(gather, "wait_send")
    last.wait()
    out_ref[...] = held[...]


def device_sum(value, axes, whole=True):
    grps = lax.axis_size(axes[1]) if whole else 1
    chips = lax.axis_size(axes[0]) // 2 * grps
    height, width = (value.shape[0], value.shape[1]) if whole else (2 * chips * value.shape[1], value.shape[2])
    half = (chips, height // (2 * chips), width)
    f32 = jnp.float32
    out = pl.pallas_call(
        functools.partial(sum_kernel, axes, grps),
        out_shape=jax.ShapeDtypeStruct((2,) + half, f32),
        in_specs=[pl.BlockSpec(memory_space=pltpu.VMEM)],
        out_specs=pl.BlockSpec(memory_space=pltpu.VMEM),
        scratch_shapes=[
            pltpu.VMEM(half, f32),
            pltpu.VMEM(half, f32),
            pltpu.VMEM(half, f32),
            pltpu.VMEM((2,) + half, f32),
            pltpu.SemaphoreType.DMA((2,)),
            pltpu.SemaphoreType.DMA((2, chips)),
            pltpu.SemaphoreType.DMA((2, chips)),
            pltpu.SemaphoreType.DMA((2,)),
        ],
        compiler_params=pltpu.CompilerParams(collective_id=0 if whole else 2, has_side_effects=True),
        name="device_sum" if whole else "far_sum",
    )(value.reshape((2,) + half) if whole else value)
    return out.reshape(height, width)


def gram_kernel(early_tiles, *refs):
    *s_refs, out_ref, raw_ref, cross_ref = refs
    step = pl.program_id(0)
    value = jnp.concatenate([s_ref[...] for s_ref in s_refs], axis=0)
    high = value.astype(jnp.bfloat16)
    rest = value - high.astype(jnp.float32)
    mid = rest.astype(jnp.bfloat16)
    low = (rest - mid.astype(jnp.float32)).astype(jnp.bfloat16)
    rows = ((0,), (0,))
    square = dot(high, high, rows, None) + dot(mid, mid, rows, None)
    cross = dot(high, mid, rows, None) + dot(high, low, rows, None)

    @pl.when(step == 0)
    def _():
        out_ref[...] = square
        cross_ref[...] = cross

    @pl.when(step > 0)
    def _():
        out_ref[...] += square
        cross_ref[...] += cross

    @pl.when(step < early_tiles)
    def _():
        raw_ref[...] = value

    @pl.when(step == pl.num_programs(0) - 1)
    def _():
        cross = cross_ref[...]
        out_ref[...] += cross + cross.T


def gram_of(snapshots, early, tile=512, streams=4):
    height, width = snapshots.shape
    early_tiles = early // tile
    return pl.pallas_call(
        functools.partial(gram_kernel, early_tiles),
        grid=(height // tile,),
        in_specs=[
            pl.BlockSpec((tile // streams, width), functools.partial(lambda q, i: (i * streams + q, 0), q))
            for q in range(streams)
        ],
        out_specs=(
            pl.BlockSpec((width, width), lambda i: (0, 0)),
            pl.BlockSpec((tile, width), lambda i: (jnp.minimum(i, early_tiles - 1), 0)),
        ),
        out_shape=(
            jax.ShapeDtypeStruct((width, width), jnp.float32),
            jax.ShapeDtypeStruct((early, width), jnp.float32),
        ),
        scratch_shapes=[pltpu.VMEM((width, width), jnp.float32)],
        compiler_params=pltpu.CompilerParams(vmem_limit_bytes=60 * 2**20),
        name="gram",
    )(*[snapshots] * streams)


def split3(value):
    high = value.astype(jnp.bfloat16)
    rest = value - high.astype(jnp.float32)
    return (high,) + split(rest)


def basis_kernel(s_ref, inverse_ref, *outs):
    sh, sm, sl = split3(s_ref[...])
    wh, wm, wl = split3(inverse_ref[...])
    plain = ((1,), (0,))
    small = dot(sl, wh, plain, None) + dot(sm, wm, plain, None) + dot(sh, wl, plain, None)
    value = small + (dot(sm, wh, plain, None) + dot(sh, wm, plain, None)) + dot(sh, wh, plain, None)
    for out in outs:
        out[...] = value.astype(out.dtype)


def basis_of(rows, inverse, start, stop, dtypes, limit=16, tile=512):
    width = rows.shape[1]
    first = start // tile
    spec = pl.BlockSpec((tile, width), lambda i: (i, 0))
    return pl.pallas_call(
        basis_kernel,
        grid=((stop - start) // tile,),
        in_specs=[
            pl.BlockSpec((tile, width), lambda i: (i + first, 0)),
            pl.BlockSpec((width, width), lambda i: (0, 0)),
        ],
        out_specs=tuple(spec for _ in dtypes),
        out_shape=tuple(jax.ShapeDtypeStruct((stop - start, width), dtype) for dtype in dtypes),
        compiler_params=pltpu.CompilerParams(vmem_limit_bytes=limit * 2**20),
        cost_estimate=pl.CostEstimate(
            flops=12 * (stop - start) * width * width,
            bytes_accessed=8 * (stop - start) * width, transcendentals=0),
        name="basis",
    )(rows, inverse)


def fill(window_ref, sems, parts, block_len):
    copies, at = [], 0
    for index, part in enumerate(parts):
        size = part.shape[0]
        copies.append(pltpu.make_async_copy(part, window_ref.at[pl.ds(at, size)], sems.at[index]))
        at += size
    for copy in copies:
        copy.start()
    window_ref[at : at + block_len] = jnp.zeros((block_len, window_ref.shape[1]), window_ref.dtype)
    for copy in copies:
        copy.wait()


def project_kernel(per_step, slots, edges, n_parts, *refs):
    places_ref, picks_ref, counts_ref = refs[:3]
    block_refs, refs = refs[3 : 3 + per_step], refs[3 + per_step :]
    basis_refs = refs[: len(edges)]
    before_ref = refs[len(edges)]
    parts = refs[1 + len(edges) : 1 + len(edges) + n_parts]
    out_ref, window_ref, image_ref, sems = refs[1 + len(edges) + n_parts :]
    step = pl.program_id(0)
    stored, block_len = block_refs[0].shape[1], block_refs[0].shape[2]

    @pl.when(step == 0)
    def _():
        out_ref[...] = before_ref[...]
        fill(window_ref, sems, parts, block_len)

    def product(r, first):
        row = step * per_step + r
        lefts, rights = [], []
        for slot in range(first, first + slots):
            at = places_ref[row, slot] * block_len
            rights.append(window_ref[pl.ds(pl.multiple_of(at, block_len), block_len), :])
            lefts.append(block_refs[r][0, slot if slots == stored else picks_ref[row, slot]])
        left = jnp.concatenate(lefts, axis=1)
        right = jnp.concatenate(rights, axis=0)
        return jnp.dot(left, right, preferred_element_type=jnp.float32)

    for r in range(per_step):
        image_ref[r * block_len : (r + 1) * block_len] = product(r, 0)
    for first in range(slots, stored, slots):
        for r in range(per_step):

            @pl.when(counts_ref[step * per_step + r, 0] > first)
            def _():
                image_ref[r * block_len : (r + 1) * block_len] += product(r, first)

    value = basis_refs[-1][...]
    for edge, ref in reversed(list(zip(edges[1:], basis_refs[:-1]))):
        value = jnp.where(step < edge, ref[...], value)
    image_high, image_low = split(image_ref[...])
    basis_high, basis_low = split(value)
    rows = ((0,), (0,))
    term = dot(basis_high, image_high, rows, None)
    term = term + dot(basis_high, image_low, rows, None)
    term = term + dot(basis_low, image_high, rows, None)
    out_ref[...] += term


def project(places, picks, counts, blocks, basis, before, parts, slots, per_step=4):
    block_rows, stored, block_len, _ = blocks.shape
    width = before.shape[1]
    depth = sum(part.shape[0] for part in parts) + block_len
    tall = per_step * block_len
    edges, specs, at = [], [], 0
    for part in basis:
        steps = part.shape[0] // tall
        edges.append(at)
        specs.append(pl.BlockSpec(
            (tall, width),
            functools.partial(lambda at, steps, i, *_: (jnp.clip(i - at, 0, steps - 1), 0), at, steps)))
        at += steps
    grid_spec = pltpu.PrefetchScalarGridSpec(
        num_scalar_prefetch=3,
        grid=(block_rows // per_step,),
        in_specs=[
            pl.BlockSpec(
                (1, stored, block_len, block_len),
                functools.partial(lambda r, i, *_: (i * per_step + r, 0, 0, 0), r))
            for r in range(per_step)
        ]
        + specs
        + [pl.BlockSpec((width, width), lambda i, *_: (0, 0))]
        + [pl.BlockSpec(memory_space=pl.ANY)] * len(parts),
        out_specs=pl.BlockSpec((width, width), lambda i, *_: (0, 0)),
        scratch_shapes=[
            pltpu.VMEM((depth, width), jnp.bfloat16),
            pltpu.VMEM((tall, width), jnp.float32),
            pltpu.SemaphoreType.DMA((len(parts),)),
        ],
    )
    return pl.pallas_call(
        functools.partial(project_kernel, per_step, slots, tuple(edges), len(parts)),
        grid_spec=grid_spec,
        out_shape=jax.ShapeDtypeStruct((width, width), jnp.float32),
        compiler_params=pltpu.CompilerParams(vmem_limit_bytes=44 * 2**20),
        cost_estimate=pl.CostEstimate(
            flops=2 * block_rows * slots * block_len * block_len * width,
            bytes_accessed=blocks.size * 2, transcendentals=0),
        name="project",
    )(places, picks, counts, *[blocks] * per_step, *basis, before, *parts)


def ring(value, axis):
    size = lax.axis_size(axis)
    for shift in range(1, size):
        yield lax.ppermute(value, axis, [((d + shift) % size, d) for d in range(size)])


def plan_kernel(size, early, columns_ref, places_ref, picks_ref, late_places_ref, counts_ref):
    block_rows, stored = columns_ref.shape
    turned = lax.rem(columns_ref[...] + (size - lax.axis_index("grp")) * block_rows, size * block_rows)
    slab, row = turned // block_rows, lax.rem(turned, block_rows)
    wanted = jnp.where((slab == 0) | (row < early), 0, 1)
    near = jnp.where(slab == 0, row, block_rows + (slab - 1) * early + row)
    places_ref[...] = jnp.where(wanted == 1, block_rows + (size - 1) * early, near)
    late = (slab - 1) * (block_rows - early) + row - early
    slot = lax.broadcasted_iota(jnp.int32, (block_rows, stored), 1)
    rank = jnp.zeros((block_rows, stored), jnp.int32)
    picks = jnp.zeros((block_rows, stored), jnp.int32)
    late_places = jnp.full((block_rows, stored), (size - 1) * (block_rows - early), jnp.int32)
    for j in range(stored):
        needs = across(wanted, j, rank.shape)
        here = (needs == 1) & (rank == slot)
        picks = jnp.where(here, j, picks)
        late_places = jnp.where(here, across(late, j, rank.shape), late_places)
        rank = rank + needs
    picks_ref[...] = picks
    late_places_ref[...] = late_places
    counts_ref[...] = rank


def plan(columns, size, early):
    return pl.pallas_call(
        functools.partial(plan_kernel, size, early),
        out_shape=(jax.ShapeDtypeStruct(columns.shape, jnp.int32),) * 4,
        name="plan",
    )(columns)


def local(snapshots, blocks, columns):
    axes = ("rows", "grp")
    height, width = snapshots.shape
    block_len, stored = blocks.shape[2], blocks.shape[1]
    size = lax.axis_size("grp")
    early = height * 3 // 8
    half, full = jnp.bfloat16, jnp.float32
    places, picks, late_places, counts = plan(columns, size, early // block_len)
    gram, raw = gram_of(snapshots, early)
    near = near_sum(gram, axes, lax.axis_size("rows") // 2)
    near, raw = lax.optimization_barrier((near, raw))
    raws = list(ring(raw, "grp"))
    factor, inverse = factorize(device_sum(near, axes, whole=False))
    cuts = (early, height)
    pieces, halves, lates = [], [], []
    for start, stop in zip(cuts[:-1], cuts[1:]):
        piece, piece_half = basis_of(snapshots, inverse, start, stop, (full, half), 60)
        pieces.append(piece)
        halves.append(piece_half)
        lates.append(list(ring(piece_half, "grp")))
    piece, piece_half = basis_of(snapshots, inverse, 0, early, (full, half))
    basis = [piece] + pieces
    first = [piece_half] + halves + [basis_of(raw, inverse, 0, early, (half,))[0] for raw in raws]
    second = [late[index] for index in range(size - 1) for late in lates]
    zero = jnp.zeros((width, width), full)
    partial_terms = project(places, picks, counts, blocks, basis, zero, first, stored)
    partial_terms = project(late_places, picks, counts, blocks, basis, partial_terms, second, stored // 2)
    projected = device_sum(partial_terms, axes)
    total_rows = height * lax.axis_size(axes)
    return projected, factor / math.sqrt(total_rows)


def solution(mesh):
    return jax.shard_map(
        local,
        mesh=mesh,
        in_specs=(
            P(("rows", "grp"), None),
            P(("rows", "grp"), None, None, None),
            P(("rows", "grp"), None),
        ),
        out_specs=(P(), P()),
        check_vma=False,
    )
```

```python
import functools
import math

import jax
import jax.numpy as jnp
from jax import lax
from jax.experimental import pallas as pl
from jax.experimental.pallas import tpu as pltpu
from jax.sharding import PartitionSpec as P

HIGHEST = lax.Precision.HIGHEST
LANES = 128
SUB = 8
MESH = pl.DeviceIdType.MESH


def dot(left, right, dims=((1,), (0,)), precision=HIGHEST):
    return lax.dot_general(
        left, right, (dims, ((), ())), precision=precision, preferred_element_type=jnp.float32
    )


def across(value, lane, shape):
    return jnp.broadcast_to(value[..., lane : lane + 1], shape)


def eliminate(head, tail):
    tiles = head.shape[0]
    one = (SUB, LANES)
    for tile in range(tiles):
        base = tile * SUB
        rows_h = [jnp.broadcast_to(head[tile, k : k + 1, :], one) for k in range(SUB)]
        rows_t = [jnp.broadcast_to(tail[tile, k : k + 1, :], one) for k in range(SUB)]
        d = {}
        for k in range(SUB):
            for i in range(k, SUB):
                d[k, i] = across(rows_h[k], base + i, one)
        later = tiles - tile - 1
        if later:
            rest_h = head[tile + 1 :]
            rest_t = tail[tile + 1 :]
            low = [across(rest_h, base + k, (later, SUB, LANES)) for k in range(SUB)]
        for k in range(SUB):
            scale = lax.rsqrt(d[k, k])
            for i in range(k + 1, SUB):
                d[k, i] = d[k, i] * scale
            rows_h[k] = rows_h[k] * scale
            rows_t[k] = rows_t[k] * scale
            for i in range(k + 1, SUB):
                for m in range(i, SUB):
                    d[i, m] = d[i, m] - d[k, i] * d[k, m]
                rows_h[i] = rows_h[i] - d[k, i] * rows_h[k]
                rows_t[i] = rows_t[i] - d[k, i] * rows_t[k]
            if later:
                low[k] = low[k] * scale[None]
                for m in range(k + 1, SUB):
                    low[m] = low[m] - low[k] * d[k, m][None]
                rest_h = rest_h - low[k] * rows_h[k][None]
                rest_t = rest_t - low[k] * rows_t[k][None]
            head[tile, k : k + 1, :] = rows_h[k][:1]
            tail[tile, k : k + 1, :] = rows_t[k][:1]
        if later:
            head[tile + 1 :] = rest_h
            tail[tile + 1 :] = rest_t


def factor_kernel(gram_ref, factor_ref, inverse_ref, head, tail):
    size = gram_ref.shape[0]
    n = LANES
    row = lax.broadcasted_iota(jnp.int32, (n, n), 0)
    col = lax.broadcasted_iota(jnp.int32, (n, n), 1)
    eye = jnp.where(row == col, 1.0, 0.0).astype(jnp.float32)
    tiles = (n // SUB, SUB, n)
    count = size // n

    for b in range(count):
        here = slice(b * n, (b + 1) * n)
        square = gram_ref[here, here]
        for a in range(b):
            above = factor_ref[a * n : (a + 1) * n, here]
            square = square - dot(above, above, ((0,), (0,)))
        head[...] = square.reshape(tiles)
        tail[...] = eye.reshape(tiles)
        eliminate(head, tail)
        lower = jnp.where(row >= col, tail[...].reshape(n, n), 0.0)
        factor_ref[here, here] = jnp.where(row <= col, head[...].reshape(n, n), 0.0)
        upper = lower.T
        inverse_ref[here, here] = upper
        for c in range(b + 1, count):
            there = slice(c * n, (c + 1) * n)
            rest = gram_ref[here, there]
            for a in range(b):
                span = slice(a * n, (a + 1) * n)
                rest = rest - dot(factor_ref[span, here], factor_ref[span, there], ((0,), (0,)))
            factor_ref[here, there] = dot(lower, rest)
            factor_ref[there, here] = jnp.zeros((n, n), jnp.float32)
            inverse_ref[there, here] = jnp.zeros((n, n), jnp.float32)
        for a in range(b):
            span = slice(a * n, (a + 1) * n)
            total = jnp.zeros((n, n), jnp.float32)
            for m in range(a, b):
                mid = slice(m * n, (m + 1) * n)
                total = total + dot(inverse_ref[span, mid], factor_ref[mid, here])
            inverse_ref[span, here] = -dot(total, upper)


def factorize(gram):
    size = gram.shape[0]
    square = jax.ShapeDtypeStruct((size, size), jnp.float32)
    return pl.pallas_call(
        factor_kernel,
        out_shape=(square, square),
        in_specs=[pl.BlockSpec(memory_space=pltpu.VMEM)],
        out_specs=(pl.BlockSpec(memory_space=pltpu.VMEM),) * 2,
        scratch_shapes=[pltpu.VMEM((LANES // SUB, SUB, LANES), jnp.float32)] * 2,
        compiler_params=pltpu.CompilerParams(vmem_limit_bytes=16 * 2**20),
        name="factorize",
    )(gram)


def split(value):
    high = value.astype(jnp.bfloat16)
    return high, (value - high.astype(jnp.float32)).astype(jnp.bfloat16)


def mate_of(axes):
    row = lax.axis_index(axes[0])
    return {axes[0]: row + 1 - 2 * lax.rem(row, 2), axes[1]: lax.axis_index(axes[1])}


def greet(barrier, where):
    pl.semaphore_signal(barrier, inc=1, device_id=where, device_id_type=MESH)


def exchange(source, target, sems, where):
    return pltpu.make_async_remote_copy(
        src_ref=source, dst_ref=target, send_sem=sems.at[0], recv_sem=sems.at[1],
        device_id=where, device_id_type=MESH)


def near_kernel(axes, grps, x_ref, out_ref, pair, own, others, pair_sems, grp_sems):
    me_row, me_grp = lax.axis_index(axes[0]), lax.axis_index(axes[1])
    core = lax.rem(me_row, 2)
    mate = mate_of(axes)
    friends = [{axes[0]: me_row, axes[1]: lax.rem(me_grp + shift, grps)} for shift in range(1, grps)]
    barrier = pltpu.get_barrier_semaphore()
    for where in [mate] + friends:
        greet(barrier, where)
    pl.semaphore_wait(barrier, grps)
    first = exchange(x_ref.at[1 - core], pair, pair_sems, mate)
    first.start()
    first.wait()
    own[...] = x_ref[core] + pair[...]
    copies = [exchange(own, others.at[i], grp_sems.at[i], where) for i, where in enumerate(friends)]
    for copy in copies:
        copy.start()
    total = own[...]
    for i, copy in enumerate(copies):
        copy.wait()
        total = total + others[i]
    out_ref[...] = total


def near_sum(value, axes, chips):
    height, width = value.shape
    grps = lax.axis_size(axes[1])
    half = (chips, height // (2 * chips), width)
    f32 = jnp.float32
    return pl.pallas_call(
        functools.partial(near_kernel, axes, grps),
        out_shape=jax.ShapeDtypeStruct(half, f32),
        in_specs=[pl.BlockSpec(memory_space=pltpu.VMEM)],
        out_specs=pl.BlockSpec(memory_space=pltpu.VMEM),
        scratch_shapes=[
            pltpu.VMEM(half, f32),
            pltpu.VMEM(half, f32),
            pltpu.VMEM((grps - 1,) + half, f32),
            pltpu.SemaphoreType.DMA((2,)),
            pltpu.SemaphoreType.DMA((grps - 1, 2)),
        ],
        compiler_params=pltpu.CompilerParams(collective_id=1, has_side_effects=True),
        name="near_sum",
    )(value.reshape((2,) + half))


def sum_kernel(axes, grps, x_ref, out_ref, pair, own, slots, held, pair_sems, scatter_sems, gather_sems, last_sems):
    rows_axis, grp_axis = axes
    chips = own.shape[0]
    me_row, me_grp = lax.axis_index(rows_axis), lax.axis_index(grp_axis)
    core = lax.rem(me_row, 2)
    mate = mate_of(axes)
    whole = grps > 1
    me = (me_row // 2) * grps + me_grp if whole else me_row // 2

    def chip(offset):
        other = lax.rem(me + offset, chips)
        if whole:
            return other, {rows_axis: (other // grps) * 2 + core, grp_axis: lax.rem(other, grps)}
        return other, {rows_axis: other * 2 + core, grp_axis: me_grp}

    barrier = pltpu.get_barrier_semaphore()
    greet(barrier, mate)

    def greet_chip(offset, carry):
        greet(barrier, chip(offset)[1])
        return carry

    lax.fori_loop(1, chips, greet_chip, 0, unroll=chips <= 16)
    pl.semaphore_wait(barrier, chips)

    if whole:
        first = exchange(x_ref.at[1 - core], pair, pair_sems, mate)
        first.start()
        first.wait()
        own[...] = x_ref[core] + pair[...]
    else:
        own[...] = x_ref[...]

    def scatter(offset):
        other, where = chip(offset)
        return pltpu.make_async_remote_copy(
            src_ref=own.at[other], dst_ref=slots.at[offset],
            send_sem=scatter_sems.at[0, offset], recv_sem=scatter_sems.at[1, offset],
            device_id=where, device_id_type=MESH)

    def gather(offset):
        _, where = chip(offset)
        return pltpu.make_async_remote_copy(
            src_ref=held.at[core, me], dst_ref=held.at[core, me],
            send_sem=gather_sems.at[0, offset], recv_sem=gather_sems.at[1, offset],
            device_id=where, device_id_type=MESH)

    def each(make, act):
        def body(offset, carry):
            getattr(make(offset), act)()
            return carry
        lax.fori_loop(1, chips, body, 0, unroll=chips <= 16)

    each(scatter, "start")
    slots[0] = own[me]
    each(scatter, "wait_recv")
    held[core, me] = jnp.sum(slots[...], axis=0)
    each(gather, "start")
    each(scatter, "wait_send")
    each(gather, "wait_recv")
    last = exchange(held.at[core], held.at[core], last_sems, mate)
    last.start()
    each(gather, "wait_send")
    last.wait()
    out_ref[...] = held[...]


def device_sum(value, axes, whole=True):
    grps = lax.axis_size(axes[1]) if whole else 1
    chips = lax.axis_size(axes[0]) // 2 * grps
    height, width = (value.shape[0], value.shape[1]) if whole else (2 * chips * value.shape[1], value.shape[2])
    half = (chips, height // (2 * chips), width)
    f32 = jnp.float32
    out = pl.pallas_call(
        functools.partial(sum_kernel, axes, grps),
        out_shape=jax.ShapeDtypeStruct((2,) + half, f32),
        in_specs=[pl.BlockSpec(memory_space=pltpu.VMEM)],
        out_specs=pl.BlockSpec(memory_space=pltpu.VMEM),
        scratch_shapes=[
            pltpu.VMEM(half, f32),
            pltpu.VMEM(half, f32),
            pltpu.VMEM(half, f32),
            pltpu.VMEM((2,) + half, f32),
            pltpu.SemaphoreType.DMA((2,)),
            pltpu.SemaphoreType.DMA((2, chips)),
            pltpu.SemaphoreType.DMA((2, chips)),
            pltpu.SemaphoreType.DMA((2,)),
        ],
        compiler_params=pltpu.CompilerParams(collective_id=0 if whole else 2, has_side_effects=True),
        name="device_sum" if whole else "far_sum",
    )(value.reshape((2,) + half) if whole else value)
    return out.reshape(height, width)


def gram_kernel(early_tiles, *refs):
    *s_refs, out_ref, raw_ref, cross_ref = refs
    step = pl.program_id(0)
    value = jnp.concatenate([s_ref[...] for s_ref in s_refs], axis=0)
    high = value.astype(jnp.bfloat16)
    rest = value - high.astype(jnp.float32)
    mid = rest.astype(jnp.bfloat16)
    low = (rest - mid.astype(jnp.float32)).astype(jnp.bfloat16)
    rows = ((0,), (0,))
    square = dot(high, high, rows, None) + dot(mid, mid, rows, None)
    cross = dot(high, mid, rows, None) + dot(high, low, rows, None)

    @pl.when(step == 0)
    def _():
        out_ref[...] = square
        cross_ref[...] = cross

    @pl.when(step > 0)
    def _():
        out_ref[...] += square
        cross_ref[...] += cross

    @pl.when(step < early_tiles)
    def _():
        raw_ref[...] = value

    @pl.when(step == pl.num_programs(0) - 1)
    def _():
        cross = cross_ref[...]
        out_ref[...] += cross + cross.T


def gram_of(snapshots, early, tile=512, streams=4):
    height, width = snapshots.shape
    early_tiles = early // tile
    return pl.pallas_call(
        functools.partial(gram_kernel, early_tiles),
        grid=(height // tile,),
        in_specs=[
            pl.BlockSpec((tile // streams, width), functools.partial(lambda q, i: (i * streams + q, 0), q))
            for q in range(streams)
        ],
        out_specs=(
            pl.BlockSpec((width, width), lambda i: (0, 0)),
            pl.BlockSpec((tile, width), lambda i: (jnp.minimum(i, early_tiles - 1), 0)),
        ),
        out_shape=(
            jax.ShapeDtypeStruct((width, width), jnp.float32),
            jax.ShapeDtypeStruct((early, width), jnp.float32),
        ),
        scratch_shapes=[pltpu.VMEM((width, width), jnp.float32)],
        compiler_params=pltpu.CompilerParams(vmem_limit_bytes=60 * 2**20),
        name="gram",
    )(*[snapshots] * streams)


def split3(value):
    high = value.astype(jnp.bfloat16)
    rest = value - high.astype(jnp.float32)
    return (high,) + split(rest)


def basis_kernel(s_ref, inverse_ref, *outs):
    sh, sm, sl = split3(s_ref[...])
    wh, wm, wl = split3(inverse_ref[...])
    plain = ((1,), (0,))
    small = dot(sl, wh, plain, None) + dot(sm, wm, plain, None) + dot(sh, wl, plain, None)
    value = small + (dot(sm, wh, plain, None) + dot(sh, wm, plain, None)) + dot(sh, wh, plain, None)
    for out in outs:
        out[...] = value.astype(out.dtype)


def basis_of(rows, inverse, start, stop, dtypes, limit=16, tile=512):
    width = rows.shape[1]
    first = start // tile
    spec = pl.BlockSpec((tile, width), lambda i: (i, 0))
    return pl.pallas_call(
        basis_kernel,
        grid=((stop - start) // tile,),
        in_specs=[
            pl.BlockSpec((tile, width), lambda i: (i + first, 0)),
            pl.BlockSpec((width, width), lambda i: (0, 0)),
        ],
        out_specs=tuple(spec for _ in dtypes),
        out_shape=tuple(jax.ShapeDtypeStruct((stop - start, width), dtype) for dtype in dtypes),
        compiler_params=pltpu.CompilerParams(vmem_limit_bytes=limit * 2**20),
        cost_estimate=pl.CostEstimate(
            flops=12 * (stop - start) * width * width,
            bytes_accessed=8 * (stop - start) * width, transcendentals=0),
        name="basis",
    )(rows, inverse)


def fill(window_ref, sems, parts, block_len):
    copies, at = [], 0
    for index, part in enumerate(parts):
        size = part.shape[0]
        copies.append(pltpu.make_async_copy(part, window_ref.at[pl.ds(at, size)], sems.at[index]))
        at += size
    for copy in copies:
        copy.start()
    window_ref[at : at + block_len] = jnp.zeros((block_len, window_ref.shape[1]), window_ref.dtype)
    for copy in copies:
        copy.wait()


def project_kernel(per_step, slots, edges, n_parts, *refs):
    places_ref, picks_ref, counts_ref = refs[:3]
    block_refs, refs = refs[3 : 3 + per_step], refs[3 + per_step :]
    basis_refs = refs[: len(edges)]
    before_ref = refs[len(edges)]
    parts = refs[1 + len(edges) : 1 + len(edges) + n_parts]
    out_ref, window_ref, image_ref, sems = refs[1 + len(edges) + n_parts :]
    step = pl.program_id(0)
    stored, block_len = block_refs[0].shape[1], block_refs[0].shape[2]

    @pl.when(step == 0)
    def _():
        out_ref[...] = before_ref[...]
        fill(window_ref, sems, parts, block_len)

    def product(r, first):
        row = step * per_step + r
        lefts, rights = [], []
        for slot in range(first, first + slots):
            at = places_ref[row, slot] * block_len
            rights.append(window_ref[pl.ds(pl.multiple_of(at, block_len), block_len), :])
            lefts.append(block_refs[r][0, slot if slots == stored else picks_ref[row, slot]])
        left = jnp.concatenate(lefts, axis=1)
        right = jnp.concatenate(rights, axis=0)
        return jnp.dot(left, right, preferred_element_type=jnp.float32)

    for r in range(per_step):
        image_ref[r * block_len : (r + 1) * block_len] = product(r, 0)
    for first in range(slots, stored, slots):
        for r in range(per_step):

            @pl.when(counts_ref[step * per_step + r, 0] > first)
            def _():
                image_ref[r * block_len : (r + 1) * block_len] += product(r, first)

    value = basis_refs[-1][...]
    for edge, ref in reversed(list(zip(edges[1:], basis_refs[:-1]))):
        value = jnp.where(step < edge, ref[...], value)
    image_high, image_low = split(image_ref[...])
    basis_high, basis_low = split(value)
    rows = ((0,), (0,))
    term = dot(basis_high, image_high, rows, None)
    term = term + dot(basis_high, image_low, rows, None)
    term = term + dot(basis_low, image_high, rows, None)
    out_ref[...] += term


def project(places, picks, counts, blocks, basis, before, parts, slots, per_step=8):
    block_rows, stored, block_len, _ = blocks.shape
    width = before.shape[1]
    depth = sum(part.shape[0] for part in parts) + block_len
    tall = per_step * block_len
    edges, specs, at = [], [], 0
    for part in basis:
        steps = part.shape[0] // tall
        edges.append(at)
        specs.append(pl.BlockSpec(
            (tall, width),
            functools.partial(lambda at, steps, i, *_: (jnp.clip(i - at, 0, steps - 1), 0), at, steps)))
        at += steps
    grid_spec = pltpu.PrefetchScalarGridSpec(
        num_scalar_prefetch=3,
        grid=(block_rows // per_step,),
        in_specs=[
            pl.BlockSpec(
                (1, stored, block_len, block_len),
                functools.partial(lambda r, i, *_: (i * per_step + r, 0, 0, 0), r))
            for r in range(per_step)
        ]
        + specs
        + [pl.BlockSpec((width, width), lambda i, *_: (0, 0))]
        + [pl.BlockSpec(memory_space=pl.ANY)] * len(parts),
        out_specs=pl.BlockSpec((width, width), lambda i, *_: (0, 0)),
        scratch_shapes=[
            pltpu.VMEM((depth, width), jnp.bfloat16),
            pltpu.VMEM((tall, width), jnp.float32),
            pltpu.SemaphoreType.DMA((len(parts),)),
        ],
    )
    return pl.pallas_call(
        functools.partial(project_kernel, per_step, slots, tuple(edges), len(parts)),
        grid_spec=grid_spec,
        out_shape=jax.ShapeDtypeStruct((width, width), jnp.float32),
        compiler_params=pltpu.CompilerParams(vmem_limit_bytes=44 * 2**20),
        cost_estimate=pl.CostEstimate(
            flops=2 * block_rows * slots * block_len * block_len * width,
            bytes_accessed=blocks.size * 2, transcendentals=0),
        name="project",
    )(places, picks, counts, *[blocks] * per_step, *basis, before, *parts)


def ring(value, axis):
    size = lax.axis_size(axis)
    for shift in range(1, size):
        yield lax.ppermute(value, axis, [((d + shift) % size, d) for d in range(size)])


def plan_kernel(size, early, columns_ref, places_ref, picks_ref, late_places_ref, counts_ref):
    block_rows, stored = columns_ref.shape
    turned = lax.rem(columns_ref[...] + (size - lax.axis_index("grp")) * block_rows, size * block_rows)
    slab, row = turned // block_rows, lax.rem(turned, block_rows)
    wanted = jnp.where((slab == 0) | (row < early), 0, 1)
    near = jnp.where(slab == 0, row, block_rows + (slab - 1) * early + row)
    places_ref[...] = jnp.where(wanted == 1, block_rows + (size - 1) * early, near)
    late = (slab - 1) * (block_rows - early) + row - early
    slot = lax.broadcasted_iota(jnp.int32, (block_rows, stored), 1)
    rank = jnp.zeros((block_rows, stored), jnp.int32)
    picks = jnp.zeros((block_rows, stored), jnp.int32)
    late_places = jnp.full((block_rows, stored), (size - 1) * (block_rows - early), jnp.int32)
    for j in range(stored):
        needs = across(wanted, j, rank.shape)
        here = (needs == 1) & (rank == slot)
        picks = jnp.where(here, j, picks)
        late_places = jnp.where(here, across(late, j, rank.shape), late_places)
        rank = rank + needs
    picks_ref[...] = picks
    late_places_ref[...] = late_places
    counts_ref[...] = rank


def plan(columns, size, early):
    return pl.pallas_call(
        functools.partial(plan_kernel, size, early),
        out_shape=(jax.ShapeDtypeStruct(columns.shape, jnp.int32),) * 4,
        name="plan",
    )(columns)


def local(snapshots, blocks, columns):
    axes = ("rows", "grp")
    height, width = snapshots.shape
    block_len, stored = blocks.shape[2], blocks.shape[1]
    size = lax.axis_size("grp")
    early = height // 2
    half, full = jnp.bfloat16, jnp.float32
    places, picks, late_places, counts = plan(columns, size, early // block_len)
    gram, raw = gram_of(snapshots, early)
    near = near_sum(gram, axes, lax.axis_size("rows") // 2)
    near, raw = lax.optimization_barrier((near, raw))
    raws = list(ring(raw, "grp"))
    factor, inverse = factorize(device_sum(near, axes, whole=False))
    cuts = (early, height)
    pieces, halves, lates = [], [], []
    for start, stop in zip(cuts[:-1], cuts[1:]):
        piece, piece_half = basis_of(snapshots, inverse, start, stop, (full, half), 60)
        pieces.append(piece)
        halves.append(piece_half)
        lates.append(list(ring(piece_half, "grp")))
    piece, piece_half = basis_of(snapshots, inverse, 0, early, (full, half))
    basis = [piece] + pieces
    first = [piece_half] + halves + [basis_of(raw, inverse, 0, early, (half,))[0] for raw in raws]
    second = [late[index] for index in range(size - 1) for late in lates]
    zero = jnp.zeros((width, width), full)
    partial_terms = project(places, picks, counts, blocks, basis, zero, first, stored)
    partial_terms = project(late_places, picks, counts, blocks, basis, partial_terms, second, stored // 2)
    projected = device_sum(partial_terms, axes)
    total_rows = height * lax.axis_size(axes)
    return projected, factor / math.sqrt(total_rows)


def solution(mesh):
    return jax.shard_map(
        local,
        mesh=mesh,
        in_specs=(
            P(("rows", "grp"), None),
            P(("rows", "grp"), None, None, None),
            P(("rows", "grp"), None),
        ),
        out_specs=(P(), P()),
        check_vma=False,
    )
```
